32 devices in a mesh: wide: 16 (over z, x, core), narrow: 2 (over y).
Axes of the slice: x: 2, y: 2, z: 4, core: 2. Of those that a mesh axis runs over, the one named last changes fastest.
Arguments:
- tokens: bfloat16 [32768, 768], P(('wide', 'narrow')), may hold values from -6 to 6
- cotangent: bfloat16 [32768, 768], P(('wide', 'narrow')), may hold values from -6 to 6
- lengths: int32 [32], P(('wide', 'narrow')), may hold values from 512 to 1024, as said below
- ln1_gain: bfloat16 [768], P(('wide', 'narrow')), may hold values from 0.099609375 to 1.8984375
- ln1_shift: bfloat16 [768], P(('wide', 'narrow')), may hold values from -3 to 3
- qkv_weight: bfloat16 [768, 2304], P(('wide', 'narrow')), may hold values from -0.21875 to 0.21875
- qkv_bias: bfloat16 [2304], P(('wide', 'narrow')), may hold values from -3 to 3
- out_weight: bfloat16 [768, 768], P(('wide', 'narrow')), may hold values from -1.25 to 1.25
- out_bias: bfloat16 [768], P(('wide', 'narrow')), may hold values from -3 to 3
- ln2_gain: bfloat16 [768], P(('wide', 'narrow')), may hold values from 0.099609375 to 1.8984375
- ln2_shift: bfloat16 [768], P(('wide', 'narrow')), may hold values from -3 to 3
- up_weight: bfloat16 [768, 3072], P(('wide', 'narrow')), may hold values from -0.21875 to 0.21875
- up_bias: bfloat16 [3072], P(('wide', 'narrow')), may hold values from -3 to 3
- down_weight: bfloat16 [3072, 768], P(('wide', 'narrow')), may hold values from -0.109375 to 0.109375
- down_bias: bfloat16 [768], P(('wide', 'narrow')), may hold values from -3 to 3
Outputs:
- mixed: bfloat16 [32768, 768], P(('wide', 'narrow'))
- grad_tokens: bfloat16 [32768, 768], P(('wide', 'narrow'))
- grad_ln1_gain: float32 [768], P(('wide', 'narrow'))
- grad_ln1_shift: float32 [768], P(('wide', 'narrow'))
- grad_qkv_weight: float32 [768, 2304], P(('wide', 'narrow'))
- grad_qkv_bias: float32 [2304], P(('wide', 'narrow'))
- grad_out_weight: float32 [768, 768], P(('wide', 'narrow'))
- grad_out_bias: float32 [768], P(('wide', 'narrow'))
- grad_ln2_gain: float32 [768], P(('wide', 'narrow'))
- grad_ln2_shift: float32 [768], P(('wide', 'narrow'))
- grad_up_weight: float32 [768, 3072], P(('wide', 'narrow'))
- grad_up_bias: float32 [3072], P(('wide', 'narrow'))
- grad_down_weight: float32 [3072, 768], P(('wide', 'narrow'))
- grad_down_bias: float32 [768], P(('wide', 'narrow'))
The draws below stay inside these ranges and needn't reach their ends.
Inputs may be any that keep to these rules, and one draw needn't show every extreme that they name: `lengths`: each value is 1024 or 512; 1024 is taken by some device in every draw.
All inputs are finite; a program needn't handle non-finite values.
Results may differ from the reference program's by a relative error of at most 0.012.
Values may be sent and summed in bfloat16 or wider, within the bound.
A program may use at most 192 MiB of HBM per device.

```python
from functools import partial
import jax
import jax.numpy as jnp
from jax import lax

D = 768
FF = 3072
HEADS = 12
HEAD = 64
ROWS = 1024
SEQS = 32
TOKENS = 32768


def draw_lengths(key, part):
    key = jax.random.fold_in(key, 7)
    bucket_key, chosen_key = jax.random.split(key)
    bucket_draw = jax.random.randint(bucket_key, (SEQS,), 0, 8)
    chosen_one = jax.random.randint(chosen_key, (), 0, SEQS)
    full_rows = (bucket_draw == 0) | (jnp.arange(SEQS, dtype=jnp.int32) == chosen_one)
    return jnp.where(full_rows, ROWS, ROWS // 2).astype(jnp.int32)


def strengthened(entries, rng, source, target, blocks, factor):
    def block_of(axis_at):
        return (jnp.arange(entries.shape[axis_at]) // (entries.shape[axis_at] // blocks)).reshape((-1,) + (1,) * (entries.ndim - 1 - axis_at))

    near = jax.random.permutation(rng, blocks)[block_of(target)]
    second = (block_of(target) + blocks // 2) % blocks
    return jnp.where((block_of(source) == near) | (block_of(source) == second), factor * entries, entries)


def block_scale(stream_key, shape, shards, smallest, largest):
    def one(dim, blocks):
        heights = jax.random.uniform(jax.random.fold_in(jax.random.fold_in(stream_key, 6), dim), (blocks,), jnp.float32, smallest / len(shards), largest / len(shards))
        return jnp.repeat(jnp.exp(heights), shape[dim] // blocks).reshape((-1,) + (1,) * (len(shape) - dim - 1))

    gain = one(*shards[0])
    for cut in shards[1:]:
        gain = gain * one(*cut)
    return gain


def bell_draw(stream_key, shape, spread, most, shards=(), held_as=jnp.bfloat16):
    gain = block_scale(stream_key, shape, shards, -0.22, 0.18) if shards else 1.0
    drawn = jax.random.normal(stream_key, shape, jnp.float32) * spread * gain
    return jnp.minimum(jnp.maximum(drawn, -most), most).astype(held_as)


def heavy_noise(key, dims, spread, most, pieces, heavy, held_as=jnp.bfloat16):
    values = spread * jax.random.normal(key, dims, jnp.float32)
    if pieces:
        values = values * block_scale(key, dims, pieces, -0.22, 0.18)
    return jnp.clip(strengthened(values, jax.random.fold_in(key, 3), *heavy), -most, most).astype(held_as)


def setup_inputs(seed: int = 0) -> dict:
    arg_keys = jax.random.split(jax.random.key(seed), 16)
    tokens = bell_draw(arg_keys[0], (TOKENS, D), 1.0, 6.0, ((0, 32),))
    cotangent = heavy_noise(arg_keys[1], (TOKENS, D), 1.0, 6.0, ((0, 32),), (0, 1, 32, 2.75))
    lengths = draw_lengths(jax.random.fold_in(arg_keys[15], 71), 0)
    ln1_gain = jnp.clip(1.0 + 0.18 * jax.random.normal(arg_keys[3], (D,), jnp.float32), 0.099609375, 1.8984375).astype(jnp.bfloat16)
    ln1_shift = bell_draw(arg_keys[4], (D,), 0.5, 3.0, ((0, 32),))
    qkv_weight = bell_draw(arg_keys[5], (D, 3 * D), D ** -0.5, 0.21875, ((0, 32),))
    qkv_bias = bell_draw(arg_keys[6], (3 * D,), 0.5, 3.0, ((0, 32),))
    out_weight = bell_draw(arg_keys[7], (D, D), (max(D // 32, 1)) ** -0.5, 1.25, ((0, 32),))
    out_bias = bell_draw(arg_keys[8], (D,), 0.5, 3.0, ((0, 32),))
    ln2_gain = jnp.clip(1.0 + 0.18 * jax.random.normal(arg_keys[9], (D,), jnp.float32), 0.099609375, 1.8984375).astype(jnp.bfloat16)
    ln2_shift = bell_draw(arg_keys[10], (D,), 0.5, 3.0, ((0, 32),))
    up_weight = bell_draw(arg_keys[11], (D, FF), D ** -0.5, 0.21875, ((0, 32),))
    up_bias = bell_draw(arg_keys[12], (FF,), 0.5, 3.0, ((0, 32),))
    down_weight = bell_draw(arg_keys[13], (FF, D), FF ** -0.5, 0.109375, ((0, 32),))
    down_bias = bell_draw(arg_keys[14], (D,), 0.5, 3.0, ((0, 32),))
    return dict(tokens=tokens, cotangent=cotangent, lengths=lengths, ln1_gain=ln1_gain, ln1_shift=ln1_shift, qkv_weight=qkv_weight, qkv_bias=qkv_bias, out_weight=out_weight, out_bias=out_bias, ln2_gain=ln2_gain, ln2_shift=ln2_shift, up_weight=up_weight, up_bias=up_bias, down_weight=down_weight, down_bias=down_bias)


@jax.custom_vjp
def low(v):
    return lax.optimization_barrier(v.astype(jnp.bfloat16)).astype(jnp.float32)

@jax.custom_vjp
def low_back(v):
    return v

def low_keep(v):
    return (low(v), None)

def low_pass(kept, grad):
    return (grad,)

def back_keep(v):
    return (v, None)

def back_low(kept, grad):
    return (low(grad),)
low.defvjp(low_keep, low_pass)
low_back.defvjp(back_keep, back_low)

def layer_norm(values, norm_gain, norm_shift):
    average = lax.optimization_barrier(jnp.mean(values, axis=-1, keepdims=True))
    centered = values - average
    variance = lax.optimization_barrier(jnp.mean(centered * centered, axis=-1, keepdims=True))
    return centered * lax.rsqrt(variance + 1e-05) * norm_gain + norm_shift

def signed_head(parts):
    query, key_rows, value_rows = parts
    scores = low_back(jnp.dot(query, key_rows.T, precision=lax.Precision.HIGHEST) * 0.125)
    length = query.shape[0]
    positions = jnp.arange(length, dtype=jnp.int32)
    causal = positions[:, None] >= positions[None, :]
    magnitude = jnp.sqrt(scores * scores + 1.0)
    masked = jnp.where(causal, magnitude, -1e+30)
    highest = lax.optimization_barrier(jnp.max(masked, axis=1, keepdims=True))
    expon = jnp.where(causal, jnp.exp(masked - highest), 0.0)
    weights = low(jnp.tanh(scores) * expon / lax.optimization_barrier(jnp.sum(expon, axis=1, keepdims=True)))
    return jnp.dot(weights, value_rows, precision=lax.Precision.HIGHEST)

def one_sequence(inputs, params):
    ln1_gain, ln1_shift, qkv_weight, qkv_bias, out_weight, out_bias, ln2_gain, ln2_shift, up_weight, up_bias, down_weight, down_bias = params
    hidden_one = low(layer_norm(inputs, ln1_gain, ln1_shift))
    qkv = low(low_back(jnp.dot(hidden_one, qkv_weight, precision=lax.Precision.HIGHEST) + qkv_bias))
    length = inputs.shape[0]
    split = qkv.reshape(length, 3, HEADS, HEAD).transpose(1, 2, 0, 3)
    head_outs = lax.map(jax.checkpoint(signed_head), (split[0], split[1], split[2]))
    attended = low(low_back(head_outs.transpose(1, 0, 2).reshape(length, D)))
    branch_one = low_back(jnp.dot(attended, out_weight, precision=lax.Precision.HIGHEST) + out_bias)
    middle = inputs + branch_one
    hidden_two = low(layer_norm(middle, ln2_gain, ln2_shift))
    upward = low_back(jnp.dot(hidden_two, up_weight, precision=lax.Precision.HIGHEST) + up_bias)
    activated = low(jax.nn.gelu(upward, approximate=True))
    branch_two = low_back(jnp.dot(activated, down_weight, precision=lax.Precision.HIGHEST) + down_bias)
    return middle + branch_two

def forward(inputs, params):
    sequences = inputs.reshape(-1, ROWS, D)
    outputs = lax.map(jax.checkpoint(partial(one_sequence, params=params)), sequences)
    return outputs.reshape(-1, D)

def reference(tokens, cotangent, lengths, ln1_gain, ln1_shift, qkv_weight, qkv_bias, out_weight, out_bias, ln2_gain, ln2_shift, up_weight, up_bias, down_weight, down_bias):
    inputs = tokens.astype(jnp.float32)
    params = (ln1_gain.astype(jnp.float32), ln1_shift.astype(jnp.float32), qkv_weight.astype(jnp.float32), qkv_bias.astype(jnp.float32), out_weight.astype(jnp.float32), out_bias.astype(jnp.float32), ln2_gain.astype(jnp.float32), ln2_shift.astype(jnp.float32), up_weight.astype(jnp.float32), up_bias.astype(jnp.float32), down_weight.astype(jnp.float32), down_bias.astype(jnp.float32))
    slots = jnp.arange(ROWS, dtype=jnp.int32)
    live = (slots[None, :] < lengths[:, None]).reshape(-1, 1)
    upstream = jnp.where(live, cotangent.astype(jnp.float32), 0.0)
    output, pullback = jax.vjp(forward, inputs, params)
    grad_inputs, grads = pullback(upstream)
    return (output.astype(jnp.bfloat16), grad_inputs.astype(jnp.bfloat16), grads[0], grads[1], grads[2], grads[3], grads[4], grads[5], grads[6], grads[7], grads[8], grads[9], grads[10], grads[11])
```

```python
import functools

import jax
import jax.numpy as jnp
from jax import lax
from jax.experimental import pallas as pl
from jax.experimental.pallas import tpu as pltpu
from jax.sharding import PartitionSpec as P

D = 768
FF = 3072
HEADS = 12
HEAD = 64
BLK = 256
AXES = ("wide", "narrow")
MESH = pl.DeviceIdType.MESH
VMEM = pltpu.VMEM
F32 = jnp.float32
BF16 = jnp.bfloat16


def nn(left, right):
    return lax.dot_general(left, right, (((1,), (0,)), ((), ())), preferred_element_type=F32)


def nt(left, right):
    return lax.dot_general(left, right, (((1,), (1,)), ((), ())), preferred_element_type=F32)


def norm_parts(values):
    average = jnp.mean(values, axis=-1, keepdims=True)
    centered = values - average
    inverse = lax.rsqrt(jnp.mean(centered * centered, axis=-1, keepdims=True) + 1e-05)
    return centered * inverse, inverse


def norm_back(grad_normed, normed, inverse):
    first_mean = jnp.mean(grad_normed, axis=-1, keepdims=True)
    second_mean = jnp.mean(grad_normed * normed, axis=-1, keepdims=True)
    return inverse * (grad_normed - first_mean - normed * second_mean)


def lane_half(values, half):
    lanes = lax.broadcasted_iota(jnp.int32, values.shape, 1)
    keep = (lanes < HEAD) if half == 0 else (lanes >= HEAD)
    return jnp.where(keep, values, jnp.zeros_like(values))


def diagonal_keep():
    keys = lax.broadcasted_iota(jnp.int32, (BLK, BLK), 0)
    queries = lax.broadcasted_iota(jnp.int32, (BLK, BLK), 1)
    return keys <= queries


def column(pair, part):
    return pl.ds(pl.multiple_of(part * D + pair * 128, 128), 128)


def qkv_rows(block, x_ref, vec24_ref, vec72_ref, wqkv_ref, qkv_ref):
    rows = pl.ds(pl.multiple_of(block * BLK, BLK), BLK)
    normed, _ = norm_parts(x_ref[rows, :].astype(F32))
    hidden = (normed * vec24_ref[0:1, :] + vec24_ref[1:2, :]).astype(BF16)
    for part in range(3):
        cols = slice(part * D, (part + 1) * D)
        qkv_ref[rows, cols] = (nn(hidden, wqkv_ref[:, cols]) + vec72_ref[6:7, cols]).astype(BF16)


def attention_pair(pair, qkv_ref, o_ref, lse_ref, vt):
    length = qkv_ref.shape[0]
    vt[...] = qkv_ref[:, column(pair, 2)].T
    keep = diagonal_keep()
    for j in range(length // BLK):
        span = (j + 1) * BLK
        rows = slice(j * BLK, span)
        query = qkv_ref[rows, column(pair, 0)] * jnp.asarray(0.125, BF16)
        keys = qkv_ref[0:span, column(pair, 1)]
        outs = []
        for half in range(2):
            s = nt(keys, lane_half(query, half))
            w = s * s + 1.0
            m = w * lax.rsqrt(w)
            tail = jnp.where(keep, m[j * BLK :], -1e30)
            m = tail if j == 0 else jnp.concatenate([m[: j * BLK], tail], axis=0)
            top = jnp.max(m, axis=0, keepdims=True)
            e = jnp.exp(m - top)
            total = jnp.sum(e, axis=0, keepdims=True)
            a = (jnp.tanh(s) * e).astype(BF16)
            outs.append(nn(vt[half * HEAD : (half + 1) * HEAD, 0:span], a) / total)
            lse_ref[pair, half : half + 1, rows] = top + jnp.log(total)
        o_ref[rows, column(pair, 0)] = jnp.concatenate(outs, axis=0).T.astype(BF16)


def attention_back_pair(pair, qkv_ref, o_ref, do_ref, lse_ref, dqkv_ref, kt, dk, dv):
    length = qkv_ref.shape[0]
    kt[...] = qkv_ref[:, column(pair, 1)].T
    keep = diagonal_keep()
    lanes = lax.broadcasted_iota(jnp.int32, (8, 128), 1)
    sublanes = lax.broadcasted_iota(jnp.int32, (8, 128), 0)
    pick = (lanes // HEAD == sublanes).astype(F32)
    steps = length // BLK
    for j in reversed(range(steps)):
        span = (j + 1) * BLK
        rows = slice(j * BLK, span)
        query = qkv_ref[rows, column(pair, 0)] * jnp.asarray(0.125, BF16)
        grad = do_ref[rows, column(pair, 0)]
        product = grad.astype(F32) * o_ref[rows, column(pair, 0)].astype(F32)
        inner = lax.dot_general(
            pick, product, (((1,), (1,)), ((), ())),
            precision=lax.Precision.HIGHEST, preferred_element_type=F32,
        )
        keys = qkv_ref[0:span, column(pair, 1)]
        values = qkv_ref[0:span, column(pair, 2)]
        dqs = []
        dks = None
        dvs = None
        for half in range(2):
            query_half = lane_half(query, half)
            grad_half = lane_half(grad, half)
            s = nt(keys, query_half)
            da = nt(values, grad_half)
            w = s * s + 1.0
            r = lax.rsqrt(w)
            p = jnp.exp(w * r - lse_ref[pair, half : half + 1, rows])
            tail = jnp.where(keep, p[j * BLK :], 0.0)
            p = tail if j == 0 else jnp.concatenate([p[: j * BLK], tail], axis=0)
            t = jnp.tanh(s)
            a = (t * p).astype(BF16)
            ds = p * (da * (1.0 - t * t) + (da * t - inner[half : half + 1, :]) * (s * r))
            ds = ds.astype(BF16)
            dqs.append(nn(kt[half * HEAD : (half + 1) * HEAD, 0:span], ds))
            this_dk = nn(ds, query_half)
            this_dv = nn(a, grad_half)
            dks = this_dk if half == 0 else dks + this_dk
            dvs = this_dv if half == 0 else dvs + this_dv
        dqkv_ref[rows, column(pair, 0)] = (jnp.concatenate(dqs, axis=0).T * 0.125).astype(BF16)
        if j == steps - 1:
            dk[...] = dks
            dv[...] = dvs
        else:
            dk[0:span, :] += dks
            dv[0:span, :] += dvs
    dqkv_ref[:, column(pair, 1)] = dk[...].astype(BF16)
    dqkv_ref[:, column(pair, 2)] = dv[...].astype(BF16)


def forward_kernel(x_ref, vec24_ref, vec72_ref, wqkv_ref, qkv_ref, o_ref, lse_ref, vt):
    lax.fori_loop(
        0,
        x_ref.shape[0] // BLK,
        lambda b, c: (qkv_rows(b, x_ref, vec24_ref, vec72_ref, wqkv_ref, qkv_ref), c)[1],
        0,
    )
    lax.fori_loop(
        0, HEADS // 2, lambda p, c: (attention_pair(p, qkv_ref, o_ref, lse_ref, vt), c)[1], 0
    )


def forward_call(x, vec24, vec72, wqkv):
    length = x.shape[0]
    return pl.pallas_call(
        forward_kernel,
        out_shape=(
            jax.ShapeDtypeStruct((length, 3 * D), BF16),
            jax.ShapeDtypeStruct((length, D), BF16),
            jax.ShapeDtypeStruct((HEADS // 2, 8, length), F32),
        ),
        in_specs=[pl.BlockSpec(memory_space=VMEM)] * 4,
        out_specs=(pl.BlockSpec(memory_space=VMEM),) * 3,
        scratch_shapes=[VMEM((128, length), BF16)],
        compiler_params=pltpu.CompilerParams(vmem_limit_bytes=56 * 2**20),
    )(x, vec24, vec72, wqkv)


def store_blocks(out_ref, first, count, value):
    depth = out_ref.shape[1]
    out_ref[pl.ds(first, count)] = value.reshape(count, depth, value.shape[1]).astype(BF16)


def middle_kernel(
    len_ref, x_ref, o_ref, cot_ref, vec24_ref, vec96_ref, wout_ref, wup_ref, wdown_ref,
    mixed_ref, do_ref, dy1_ref, gout_ref, gup_ref, gdown_ref, small24_ref, small96_ref,
    f_t, du, h2_t, dy, dz, o_t,
):
    step = pl.program_id(0)
    steps = pl.num_programs(0)
    rows_at = pl.multiple_of(step * BLK, BLK)
    here = pl.ds(rows_at, BLK)
    chunk = 768

    @pl.when(step == 0)
    def _():
        small24_ref[...] = jnp.zeros_like(small24_ref)
        small96_ref[...] = jnp.zeros_like(small96_ref)

    attended = o_ref[...]
    y1 = x_ref[...].astype(F32) + nn(attended, wout_ref[...]) + vec24_ref[2:3, :]
    normed, inverse = norm_parts(y1)
    h2 = (normed * vec24_ref[3:4, :] + vec24_ref[4:5, :]).astype(BF16)
    rows = lax.broadcasted_iota(jnp.int32, (BLK, D), 0) + rows_at
    upstream = jnp.where(rows < len_ref[0], cot_ref[...].astype(F32), 0.0)
    upstream16 = upstream.astype(BF16)
    y = y1 + vec24_ref[5:6, :]
    dh2 = None
    for c in range(FF // chunk):
        cols = slice(c * chunk, (c + 1) * chunk)
        u = nn(h2, wup_ref[:, cols]) + vec96_ref[7:8, cols]
        square = u * u
        t = jnp.tanh(u * (0.7978845608028654 + 0.035677408136300125 * square))
        half = 0.5 * (1.0 + t)
        f = (u * half).astype(BF16)
        slope = half + (0.5 * u) * (1.0 - t * t) * (
            0.7978845608028654 + 0.10703222440890037 * square
        )
        y = y + nn(f, wdown_ref[cols, :])
        df = nt(upstream16, wdown_ref[cols, :])
        d16 = (df * slope).astype(BF16)
        du[here, cols] = d16
        f_t[cols, here] = f.T
        small96_ref[7:8, cols] += jnp.sum(d16.astype(F32), axis=0, keepdims=True)
        part = nt(d16, wup_ref[:, cols])
        dh2 = part if c == 0 else dh2 + part
    mixed_ref[...] = y.astype(BF16)
    e = dh2 * vec24_ref[3:4, :]
    dy1 = upstream + norm_back(e, normed, inverse)
    dz16 = dy1.astype(BF16)
    dy1_ref[...] = dy1
    do_ref[...] = nt(dz16, wout_ref[...]).astype(BF16)
    small24_ref[2:3, :] += jnp.sum(dz16.astype(F32), axis=0, keepdims=True)
    small24_ref[3:4, :] += jnp.sum(dh2 * normed, axis=0, keepdims=True)
    small24_ref[4:5, :] += jnp.sum(dh2, axis=0, keepdims=True)
    small24_ref[5:6, :] += jnp.sum(upstream, axis=0, keepdims=True)
    h2_t[:, here] = h2.T
    o_t[:, here] = attended.T
    dy[here, :] = upstream16
    dz[here, :] = dz16

    @pl.when(step == steps - 1)
    def _():
        shards = gout_ref.shape[0]
        many = shards // 4
        deep = gdown_ref.shape[1] * many // 4

        def one(i, carry):
            first = pl.multiple_of(i * many, many)
            left = pl.ds(pl.multiple_of(i * (D // 4), D // 4), D // 4)
            store_blocks(gout_ref, first, many, nn(o_t[left, :], dz[...]))
            for c in range(FF // chunk):
                cols = slice(c * chunk, (c + 1) * chunk)
                value = nn(h2_t[left, :], du[:, cols]).reshape(many, D // shards, chunk)
                gup_ref[pl.ds(first, many), :, cols] = value.astype(BF16)
            return carry

        lax.fori_loop(0, 4, one, 0)

        def two(i, carry):
            left = pl.ds(pl.multiple_of(i * deep, deep), deep)
            store_blocks(gdown_ref, i * (many // 4), many // 4, nn(f_t[left, :], dy[...]))
            return carry

        lax.fori_loop(0, 16, two, 0)


def middle_call(lengths, x, attended, cotangent, vec24, vec96, wout, wup, wdown, shards):
    length = x.shape[0]

    def rows(width):
        return pl.BlockSpec((BLK, width), lambda i: (i, 0))

    def whole(shape):
        return pl.BlockSpec(
            shape, lambda i: (0,) * len(shape), pipeline_mode=pl.Buffered(1)
        )

    outs = (
        ((length, D), BF16, rows(D)),
        ((length, D), BF16, rows(D)),
        ((length, D), F32, rows(D)),
        ((shards, D // shards, D), BF16, None),
        ((shards, D // shards, FF), BF16, None),
        ((shards, FF // shards, D), BF16, None),
        ((16, D), F32, None),
        ((16, FF), F32, None),
    )
    return pl.pallas_call(
        middle_kernel,
        grid=(length // BLK,),
        out_shape=tuple(jax.ShapeDtypeStruct(s, t) for s, t, _ in outs),
        in_specs=[
            pl.BlockSpec(memory_space=pltpu.SMEM),
            rows(D), rows(D), rows(D),
            whole(vec24.shape), whole(vec96.shape),
            whole(wout.shape), whole(wup.shape), whole(wdown.shape),
        ],
        out_specs=tuple(whole(s) if b is None else b for s, _, b in outs),
        scratch_shapes=[
            VMEM((FF, length), BF16),
            VMEM((length, FF), BF16),
            VMEM((D, length), BF16),
            VMEM((length, D), BF16),
            VMEM((length, D), BF16),
            VMEM((D, length), BF16),
        ],
        compiler_params=pltpu.CompilerParams(
            dimension_semantics=("arbitrary",), vmem_limit_bytes=60 * 2**20
        ),
    )(lengths, x, attended, cotangent, vec24, vec96, wout, wup, wdown)


def tail_rows(block, x_ref, dy1_ref, vec24_ref, wqkv_ref, dqkv_ref, h1_t, gx_ref, s24_ref, s72_ref):
    here = pl.ds(pl.multiple_of(block * BLK, BLK), BLK)
    normed, inverse = norm_parts(x_ref[here, :].astype(F32))
    hidden = (normed * vec24_ref[0:1, :] + vec24_ref[1:2, :]).astype(BF16)
    h1_t[:, here] = hidden.T
    grad = dqkv_ref[here, :]
    dh1 = nt(grad, wqkv_ref[...])
    e = dh1 * vec24_ref[0:1, :]
    gx_ref[here, :] = (dy1_ref[here, :] + norm_back(e, normed, inverse)).astype(BF16)
    s24_ref[0:1, :] += jnp.sum(dh1 * normed, axis=0, keepdims=True)
    s24_ref[1:2, :] += jnp.sum(dh1, axis=0, keepdims=True)
    s72_ref[6:7, :] += jnp.sum(grad.astype(F32), axis=0, keepdims=True)


def backward_kernel(
    x_ref, dy1_ref, vec24_ref, wqkv_ref, qkv_ref, o_ref, do_ref, lse_ref,
    gx_ref, gqkv_ref, s24_ref, s72_ref,
    dqkv, h1_t, kt, dk, dv,
):
    s24_ref[...] = jnp.zeros_like(s24_ref)
    s72_ref[...] = jnp.zeros_like(s72_ref)
    lax.fori_loop(
        0,
        HEADS // 2,
        lambda p, c: (
            attention_back_pair(p, qkv_ref, o_ref, do_ref, lse_ref, dqkv, kt, dk, dv),
            c,
        )[1],
        0,
    )
    lax.fori_loop(
        0,
        x_ref.shape[0] // BLK,
        lambda b, c: (
            tail_rows(
                b, x_ref, dy1_ref, vec24_ref, wqkv_ref, dqkv, h1_t, gx_ref, s24_ref, s72_ref
            ),
            c,
        )[1],
        0,
    )
    shards = gqkv_ref.shape[0]
    many = shards // 4

    def one(i, carry):
        left = pl.ds(pl.multiple_of(i * (D // 4), D // 4), D // 4)
        for part in range(3):
            cols = slice(part * D, (part + 1) * D)
            value = nn(h1_t[left, :], dqkv[:, cols]).reshape(many, D // shards, D)
            gqkv_ref[pl.ds(i * many, many), :, cols] = value.astype(BF16)
        return carry

    lax.fori_loop(0, 4, one, 0)


def backward_call(x, dy1, vec24, wqkv, qkv, attended, grad_attended, lse, shards):
    length = x.shape[0]
    return pl.pallas_call(
        backward_kernel,
        out_shape=(
            jax.ShapeDtypeStruct((length, D), BF16),
            jax.ShapeDtypeStruct((shards, D // shards, 3 * D), BF16),
            jax.ShapeDtypeStruct((16, D), F32),
            jax.ShapeDtypeStruct((16, 3 * D), F32),
        ),
        in_specs=[pl.BlockSpec(memory_space=VMEM)] * 8,
        out_specs=(pl.BlockSpec(memory_space=VMEM),) * 4,
        scratch_shapes=[
            VMEM((length, 3 * D), BF16),
            VMEM((D, length), BF16),
            VMEM((128, length), BF16),
            VMEM((length, 128), F32),
            VMEM((length, 128), F32),
        ],
        compiler_params=pltpu.CompilerParams(vmem_limit_bytes=60 * 2**20),
    )(x, dy1, vec24, wqkv, qkv, attended, grad_attended, lse)


def place():
    wide = lax.axis_index("wide")
    return wide // 4, (wide // 2) % 2, wide % 2, lax.axis_index("narrow")


def device(z, x, c, y):
    return ((z * 2 + x) * 2 + c, y)


def greet():
    z, x, c, y = place()
    barrier = pltpu.get_barrier_semaphore()
    peers = [device(lax.rem(z + d, 4), x, c, y) for d in (1, 2, 3)]
    peers += [device(z, 1 - x, c, y), device(z, x, c, 1 - y), device(z, x, 1 - c, y)]
    for peer in peers:
        pl.semaphore_signal(barrier, inc=1, device_id=peer, device_id_type=MESH)
    pl.semaphore_wait(barrier, len(peers))


def remote(src, dst, sems, slot, peer):
    return pltpu.make_async_remote_copy(
        src_ref=src, dst_ref=dst, send_sem=sems[0].at[slot], recv_sem=sems[1].at[slot],
        device_id=peer, device_id_type=MESH,
    )


class Gather:
    slots = 12

    def __init__(self, own, full, sems, local_sem):
        self.own, self.full, self.sems, self.local = own, full, sems, local_sem
        width = full.shape[-1]
        cut = width // 256 * 128
        self.first = pl.ds(0, cut or width)
        self.second = pl.ds(cut, width - cut) if cut else None
        z, x, c, y = place()
        self.peer_x = device(z, 1 - x, c, y)
        self.peer_y = device(z, x, c, 1 - y)
        self.peer_c = device(z, x, 1 - c, y)
        self.at = (z, x, c, y)
        self.copies = []

    def send(self, slot, peer, *index):
        view = self.full.at[index]
        copy = remote(view, view, self.sems, slot, peer)
        copy.start()
        self.copies.append(copy)
        return copy

    def stage0(self):
        z, x, c, y = self.at
        target = self.full.at[z, x, c, y]
        self.keep = pltpu.make_async_copy(self.own, target, self.local)
        self.keep.start()
        self.pending = []
        for d in (2, 1, 3):
            copy = remote(self.own, target, self.sems, d - 1, device(lax.rem(z + d, 4), x, c, y))
            copy.start()
            self.copies.append(copy)
            self.pending.append(copy)

    def land(self):
        for copy in self.pending:
            copy.wait_recv()
        self.pending = []

    def stage1(self):
        z, x, c, y = self.at
        self.keep.wait()
        self.land()
        every = slice(None)
        self.pending = [self.send(3, self.peer_x, every, x, c, y, every, self.first)]
        if self.second is not None:
            self.pending.append(self.send(4, self.peer_y, every, x, c, y, every, self.second))
        self.core = [self.send(5, self.peer_c, every, x, c, y)]

    def stage2(self):
        z, x, c, y = self.at
        self.land()
        every = slice(None)
        self.pending = [self.send(6, self.peer_y, every, every, c, y, every, self.first)]
        self.core.append(self.send(7, self.peer_c, every, 1 - x, c, y, every, self.first))
        if self.second is not None:
            self.pending.append(self.send(8, self.peer_x, every, x, c, every, every, self.second))
            self.core.append(self.send(9, self.peer_c, every, x, c, 1 - y, every, self.second))

    def stage3(self):
        z, x, c, y = self.at
        self.land()
        every = slice(None)
        self.core.append(self.send(10, self.peer_c, every, every, c, 1 - y, every, self.first))
        if self.second is not None:
            self.core.append(self.send(11, self.peer_c, every, 1 - x, c, every, every, self.second))

    def stage4(self):
        for copy in self.core:
            copy.wait_recv()

    def finish(self):
        for copy in self.copies:
            copy.wait_send()


def spread(blocks, each):
    width = 32 * each
    lane = lax.broadcasted_iota(jnp.int32, (128, width), 0)
    col = lax.broadcasted_iota(jnp.int32, (128, width), 1)
    value = nn(blocks, (lax.rem(col, each) == lane).astype(BF16)).reshape(32, 16, width)
    shard = lax.broadcasted_iota(jnp.int32, (32, 16, width), 0)
    col = lax.broadcasted_iota(jnp.int32, (32, 16, width), 2)
    inside = (col >= shard * each) & (col < shard * each + each)
    return jnp.sum(jnp.where(inside, value, 0.0), axis=0)


def gather_kernel(small, wqkv, wout, wup, wdown, *refs):
    full = refs[1:5]
    vec_refs = refs[5:8]
    small_full = refs[0]
    send, recv, local = refs[8:11]
    greet()
    parts = []
    for i, (own, out) in enumerate(zip((small, wqkv, wout, wup, wdown), (small_full, *full))):
        parts.append(Gather(own, out, (send.at[i], recv.at[i]), local.at[i]))
    for stage in ("stage0", "stage1", "stage2", "stage3", "stage4", "finish"):
        for part in parts:
            getattr(part, stage)()
    blocks = small_full[...].reshape(32 * 16, 128)
    for ref, each in zip(vec_refs, (24, 72, 96)):
        ref[...] = spread(blocks, each)


def gather_call(small, wqkv, wout, wup, wdown):
    own = (small, wqkv, wout, wup, wdown)
    full = tuple(jax.ShapeDtypeStruct((4, 2, 2, 2, *a.shape), BF16) for a in own)
    anywhere = pl.BlockSpec(memory_space=pl.ANY)
    inside = pl.BlockSpec(memory_space=VMEM)
    return pl.pallas_call(
        gather_kernel,
        out_shape=(
            *full,
            jax.ShapeDtypeStruct((16, D), F32),
            jax.ShapeDtypeStruct((16, 3 * D), F32),
            jax.ShapeDtypeStruct((16, FF), F32),
        ),
        in_specs=[inside] + [anywhere] * 4,
        out_specs=(inside, *[anywhere] * 4, *[inside] * 3),
        scratch_shapes=[
            pltpu.SemaphoreType.DMA((5, Gather.slots)),
            pltpu.SemaphoreType.DMA((5, Gather.slots)),
            pltpu.SemaphoreType.DMA((5,)),
        ],
        compiler_params=pltpu.CompilerParams(
            collective_id=1, has_side_effects=True, vmem_limit_bytes=40 * 2**20
        ),
    )(*own)


class Scatter:
    slots = 11

    def __init__(self, grads, out, buffers, sems):
        self.grads, self.out, self.sems = grads, out, sems
        self.one, self.two, self.three, self.four = buffers
        width = grads.shape[-1]
        cut = width // 256 * 128
        self.first = pl.ds(0, cut or width)
        self.second = pl.ds(cut, width - cut) if cut else None
        z, x, c, y = place()
        self.peer_x = device(z, 1 - x, c, y)
        self.peer_y = device(z, x, c, 1 - y)
        self.peer_c = device(z, x, 1 - c, y)
        self.at = (z, x, c, y)
        self.copies = []
        self.pending = []

    @staticmethod
    def shapes(r, n):
        return [
            VMEM((4, 2, 2, r, n), BF16),
            VMEM((4, 2, r, n), BF16),
            VMEM((4, r, n), BF16),
            VMEM((3, r, n), BF16),
        ]

    def send(self, slot, peer, src, dst):
        copy = remote(src, dst, self.sems, slot, peer)
        copy.start()
        self.copies.append(copy)
        self.pending.append(copy)

    def land(self):
        for copy in self.pending:
            copy.wait_recv()
        self.pending = []

    def stage0(self):
        c = self.at[2]
        self.send(0, self.peer_c, self.grads.at[:, :, 1 - c], self.one)

    def stage1(self):
        z, x, c, y = self.at
        self.land()

        def add(i, carry):
            a, b = i // 2, i % 2
            self.one[a, b] = (
                self.one[a, b].astype(F32) + self.grads[a, b, c].astype(F32)
            ).astype(BF16)
            return carry

        lax.fori_loop(0, 8, add, 0)
        every = slice(None)
        self.send(
            1, self.peer_x, self.one.at[:, 1 - x, :, :, self.first],
            self.two.at[:, :, :, self.first],
        )
        if self.second is not None:
            self.send(
                2, self.peer_y, self.one.at[:, :, 1 - y, :, self.second],
                self.two.at[:, :, :, self.second],
            )

    def stage2(self):
        z, x, c, y = self.at
        self.land()

        def add(a, carry):
            cols = self.first
            self.two[a, :, :, cols] = (
                self.two[a, :, :, cols].astype(F32) + self.one[a, x, :, :, cols].astype(F32)
            ).astype(BF16)
            if self.second is not None:
                cols = self.second
                for b in range(2):
                    self.two[a, b, :, cols] = (
                        self.two[a, b, :, cols].astype(F32) + self.one[a, b, y, :, cols].astype(F32)
                    ).astype(BF16)
            return carry

        lax.fori_loop(0, 4, add, 0)
        self.send(
            3, self.peer_y, self.two.at[:, 1 - y, :, self.first], self.three.at[:, :, self.first]
        )
        if self.second is not None:
            self.send(
                4, self.peer_x, self.two.at[:, 1 - x, :, self.second],
                self.three.at[:, :, self.second],
            )

    def stage3(self):
        z, x, c, y = self.at
        self.land()

        def add(a, carry):
            for cols, which in ((self.first, y), (self.second, x)):
                if cols is not None:
                    self.three[a, :, cols] = (
                        self.three[a, :, cols].astype(F32) + self.two[a, which, :, cols].astype(F32)
                    ).astype(BF16)
            return carry

        lax.fori_loop(0, 4, add, 0)
        for d in (2, 1, 3):
            other = lax.rem(z + d, 4)
            self.send(4 + d, device(other, x, c, y), self.three.at[other], self.four.at[d - 1])

    def stage4(self):
        z = self.at[0]
        self.land()
        self.out[...] = (
            self.three[z].astype(F32)
            + self.four[0].astype(F32)
            + self.four[1].astype(F32)
            + self.four[2].astype(F32)
        )
        for copy in self.copies:
            copy.wait_send()


def fold(values, each, row):
    width = 32 * each
    shard = lax.broadcasted_iota(jnp.int32, (32, 16, width), 0)
    col = lax.broadcasted_iota(jnp.int32, (32, 16, width), 2)
    inside = (col >= shard * each) & (col < shard * each + each)
    spreaded = jnp.where(inside, values[None], 0.0).reshape(32 * 16, width).astype(BF16)
    lane = lax.broadcasted_iota(jnp.int32, (128, width), 0)
    col = lax.broadcasted_iota(jnp.int32, (128, width), 1)
    return nt(spreaded, (lax.rem(col, each) == lane).astype(BF16))


def scatter_kernel(count, *refs):
    grads = refs[:count]
    smalls = refs[count : count + 4]
    outs = refs[count + 4 : 2 * count + 5]
    buffers = refs[2 * count + 5 :]
    small_grads = buffers[0]
    buffers = buffers[1:]
    send, recv = buffers[-2:]
    greet()
    parts = []
    for i in range(count + 1):
        own = grads[i] if i < count else small_grads
        parts.append(Scatter(own, outs[i], buffers[4 * i : 4 * i + 4], (send.at[i], recv.at[i])))
    for part in parts[:-1]:
        part.stage0()
    total = fold(smalls[0][...] + smalls[1][...], 24, 0)
    total = total + fold(smalls[2][...], 72, 6) + fold(smalls[3][...], 96, 7)
    small_grads[...] = total.reshape(4, 2, 2, 2, 16, 128).astype(BF16)
    parts[-1].stage0()
    for stage in ("stage1", "stage2", "stage3", "stage4"):
        for part in parts:
            getattr(part, stage)()


def scatter_call(grads, smalls):
    inside = pl.BlockSpec(memory_space=VMEM)
    shapes = [g.shape[-2:] for g in grads] + [(16, 128)]
    scratch = [VMEM((4, 2, 2, 2, 16, 128), BF16)]
    for r, n in shapes:
        scratch += Scatter.shapes(r, n)
    scratch += [pltpu.SemaphoreType.DMA((len(shapes), Scatter.slots))] * 2
    return pl.pallas_call(
        functools.partial(scatter_kernel, len(grads)),
        out_shape=tuple(jax.ShapeDtypeStruct(s, F32) for s in shapes),
        in_specs=[inside] * (len(grads) + 4),
        out_specs=(inside,) * len(shapes),
        scratch_shapes=scratch,
        compiler_params=pltpu.CompilerParams(
            collective_id=2, has_side_effects=True, vmem_limit_bytes=60 * 2**20
        ),
    )(*grads, *smalls)


def shards(
    tokens, cotangent, lengths, ln1_gain, ln1_shift, qkv_weight, qkv_bias, out_weight, out_bias,
    ln2_gain, ln2_shift, up_weight, up_bias, down_weight, down_bias, *, special,
):
    vectors = (ln1_gain, ln1_shift, out_bias, ln2_gain, ln2_shift, down_bias, qkv_bias, up_bias)
    if special:
        small = jnp.stack(
            [jnp.pad(v, (0, 128 - v.shape[0])) for v in vectors] + [jnp.zeros((128,), BF16)] * 8
        )
        _, wqkv, wout, wup, wdown, vec24, vec72, vec96 = gather_call(
            small, qkv_weight, out_weight, up_weight, down_weight
        )
        wqkv, wout, wup = (w.reshape(D, w.shape[-1]) for w in (wqkv, wout, wup))
        wdown = wdown.reshape(FF, D)
    else:
        gather = functools.partial(lax.all_gather, axis_name=AXES, axis=0, tiled=True)
        wqkv, wout, wup, wdown = map(gather, (qkv_weight, out_weight, up_weight, down_weight))
        whole = [gather(v).astype(F32) for v in vectors]
        vec24 = jnp.pad(jnp.stack(whole[:6]), ((0, 10), (0, 0)))
        vec72 = jnp.pad(whole[6][None], ((6, 9), (0, 0)))
        vec96 = jnp.pad(whole[7][None], ((7, 8), (0, 0)))
    qkv, attended, lse = forward_call(tokens, vec24, vec72, wqkv)
    mixed, do, dy1, gout, gup, gdown, s24_mid, s96 = middle_call(
        lengths, tokens, attended, cotangent, vec24, vec96, wout, wup, wdown, 32
    )
    gx, gqkv, s24, s72 = backward_call(tokens, dy1, vec24, wqkv, qkv, attended, do, lse, 32)
    if special:
        blocks = [g.reshape(4, 2, 2, 2, *g.shape[1:]) for g in (gqkv, gout, gup, gdown)]
        gqkv, gout, gup, gdown, small = scatter_call(blocks, (s24, s24_mid, s72, s96))
        sizes = [v.shape[0] for v in vectors]
        folded = [small[i, :n] for i, n in enumerate(sizes)]
    else:
        scatter = functools.partial(
            lax.psum_scatter, axis_name=AXES, scatter_dimension=0, tiled=True
        )
        gqkv, gout, gup = (scatter(g.reshape(D, -1).astype(F32)) for g in (gqkv, gout, gup))
        gdown = scatter(gdown.reshape(FF, D).astype(F32))
        both = s24 + s24_mid
        folded = [scatter(both[i]) for i in range(6)] + [scatter(s72[6]), scatter(s96[7])]
    return (
        mixed, gx, folded[0], folded[1], gqkv, folded[6], gout, folded[2], folded[3], folded[4],
        gup, folded[7], gdown, folded[5],
    )


def solution(mesh):
    flat, rows = P(AXES), P(AXES, None)
    in_specs = (
        rows, rows, flat, flat, flat, rows, flat, rows, flat, flat, flat, rows, flat, rows, flat,
    )
    out_specs = (
        rows, rows, flat, flat, rows, flat, rows, flat, flat, flat, rows, flat, rows, flat,
    )
    special = dict(mesh.shape) == {"wide": 16, "narrow": 2}
    return jax.shard_map(
        functools.partial(shards, special=special),
        mesh=mesh, in_specs=in_specs, out_specs=out_specs, check_vma=False,
    )
```

```python
import functools

import jax
import jax.numpy as jnp
from jax import lax
from jax.experimental import pallas as pl
from jax.experimental.pallas import tpu as pltpu
from jax.sharding import PartitionSpec as P

D = 768
FF = 3072
HEADS = 12
HEAD = 64
BLK = 256
MID = 256
CHUNK = 768
AXES = ("wide", "narrow")
MESH = pl.DeviceIdType.MESH
VMEM = pltpu.VMEM
F32 = jnp.float32
BF16 = jnp.bfloat16


def nn(left, right):
    return lax.dot_general(left, right, (((1,), (0,)), ((), ())), preferred_element_type=F32)


def nt(left, right):
    return lax.dot_general(left, right, (((1,), (1,)), ((), ())), preferred_element_type=F32)


def norm_parts(values):
    average = jnp.mean(values, axis=-1, keepdims=True)
    centered = values - average
    inverse = lax.rsqrt(jnp.mean(centered * centered, axis=-1, keepdims=True) + 1e-05)
    return centered * inverse, inverse


def norm_back(grad_normed, normed, inverse):
    first_mean = jnp.mean(grad_normed, axis=-1, keepdims=True)
    second_mean = jnp.mean(grad_normed * normed, axis=-1, keepdims=True)
    return inverse * (grad_normed - first_mean - normed * second_mean)


def lane_half(values, half):
    lanes = lax.broadcasted_iota(jnp.int32, values.shape, 1)
    keep = (lanes < HEAD) if half == 0 else (lanes >= HEAD)
    return jnp.where(keep, values, jnp.zeros_like(values))


def diagonal_keep():
    keys = lax.broadcasted_iota(jnp.int32, (BLK, BLK), 0)
    queries = lax.broadcasted_iota(jnp.int32, (BLK, BLK), 1)
    return keys <= queries


def column(pair, part):
    return pl.ds(pl.multiple_of(part * D + pair * 128, 128), 128)


def qkv_rows(block, x_ref, vec24_ref, vec72_ref, wqkv_ref, qkv_ref):
    rows = pl.ds(pl.multiple_of(block * BLK, BLK), BLK)
    normed, _ = norm_parts(x_ref[rows, :].astype(F32))
    hidden = (normed * vec24_ref[0:1, :] + vec24_ref[1:2, :]).astype(BF16)
    for part in range(3):
        cols = slice(part * D, (part + 1) * D)
        qkv_ref[rows, cols] = (nn(hidden, wqkv_ref[:, cols]) + vec72_ref[6:7, cols]).astype(BF16)


def attention_pair(pair, qkv_ref, o_ref, lse_ref, vt, event=lambda j: None):
    length = qkv_ref.shape[0]
    vt[...] = qkv_ref[:, column(pair, 2)].T
    keep = diagonal_keep()
    for j in range(length // BLK):
        event(j)
        span = (j + 1) * BLK
        rows = slice(j * BLK, span)
        query = qkv_ref[rows, column(pair, 0)] * jnp.asarray(0.125, BF16)
        keys = qkv_ref[0:span, column(pair, 1)]
        outs = []
        for half in range(2):
            s = nt(keys, lane_half(query, half))
            w = s * s + 1.0
            m = w * lax.rsqrt(w)
            tail = jnp.where(keep, m[j * BLK :], -1e30)
            m = tail if j == 0 else jnp.concatenate([m[: j * BLK], tail], axis=0)
            top = jnp.max(m, axis=0, keepdims=True)
            e = jnp.exp(m - top)
            total = jnp.sum(e, axis=0, keepdims=True)
            a = (jnp.tanh(s) * e).astype(BF16)
            outs.append(nn(vt[half * HEAD : (half + 1) * HEAD, 0:span], a) / total)
            lse_ref[pair, half : half + 1, rows] = top + jnp.log(total)
        o_ref[rows, column(pair, 0)] = jnp.concatenate(outs, axis=0).T.astype(BF16)


def attention_back_pair(
    pair, qkv_ref, o_ref, do_ref, lse_ref, dqkv_ref, kt, dk, dv, event=lambda j: None
):
    length = qkv_ref.shape[0]
    kt[...] = qkv_ref[:, column(pair, 1)].T
    keep = diagonal_keep()
    lanes = lax.broadcasted_iota(jnp.int32, (8, 128), 1)
    sublanes = lax.broadcasted_iota(jnp.int32, (8, 128), 0)
    pick = (lanes // HEAD == sublanes).astype(F32)
    steps = length // BLK
    for j in reversed(range(steps)):
        event(j)
        span = (j + 1) * BLK
        rows = slice(j * BLK, span)
        query = qkv_ref[rows, column(pair, 0)] * jnp.asarray(0.125, BF16)
        grad = do_ref[rows, column(pair, 0)]
        product = grad.astype(F32) * o_ref[rows, column(pair, 0)].astype(F32)
        inner = lax.dot_general(
            pick, product, (((1,), (1,)), ((), ())),
            precision=lax.Precision.HIGHEST, preferred_element_type=F32,
        )
        keys = qkv_ref[0:span, column(pair, 1)]
        values = qkv_ref[0:span, column(pair, 2)]
        dqs = []
        dks = None
        dvs = None
        for half in range(2):
            query_half = lane_half(query, half)
            grad_half = lane_half(grad, half)
            s = nt(keys, query_half)
            da = nt(values, grad_half)
            w = s * s + 1.0
            r = lax.rsqrt(w)
            p = jnp.exp(w * r - lse_ref[pair, half : half + 1, rows])
            tail = jnp.where(keep, p[j * BLK :], 0.0)
            p = tail if j == 0 else jnp.concatenate([p[: j * BLK], tail], axis=0)
            t = jnp.tanh(s)
            a = (t * p).astype(BF16)
            ds = p * (da * (1.0 - t * t) + (da * t - inner[half : half + 1, :]) * (s * r))
            ds = ds.astype(BF16)
            dqs.append(nn(kt[half * HEAD : (half + 1) * HEAD, 0:span], ds))
            this_dk = nn(ds, query_half)
            this_dv = nn(a, grad_half)
            dks = this_dk if half == 0 else dks + this_dk
            dvs = this_dv if half == 0 else dvs + this_dv
        dqkv_ref[rows, column(pair, 0)] = (jnp.concatenate(dqs, axis=0).T * 0.125).astype(BF16)
        if j == steps - 1:
            dk[...] = dks
            dv[...] = dvs
        else:
            dk[0:span, :] += dks
            dv[0:span, :] += dvs
    dqkv_ref[:, column(pair, 1)] = dk[...].astype(BF16)
    dqkv_ref[:, column(pair, 2)] = dv[...].astype(BF16)


def forward_kernel(x_ref, vec24_ref, vec72_ref, wqkv_ref, qkv_ref, o_ref, lse_ref, vt):
    lax.fori_loop(
        0,
        x_ref.shape[0] // BLK,
        lambda b, c: (qkv_rows(b, x_ref, vec24_ref, vec72_ref, wqkv_ref, qkv_ref), c)[1],
        0,
    )
    lax.fori_loop(
        0, HEADS // 2, lambda p, c: (attention_pair(p, qkv_ref, o_ref, lse_ref, vt), c)[1], 0
    )


def forward_call(x, vec24, vec72, wqkv):
    length = x.shape[0]
    return pl.pallas_call(
        forward_kernel,
        out_shape=(
            jax.ShapeDtypeStruct((length, 3 * D), BF16),
            jax.ShapeDtypeStruct((length, D), BF16),
            jax.ShapeDtypeStruct((HEADS // 2, 8, length), F32),
        ),
        in_specs=[pl.BlockSpec(memory_space=VMEM)] * 4,
        out_specs=(pl.BlockSpec(memory_space=VMEM),) * 3,
        scratch_shapes=[VMEM((128, length), BF16)],
        compiler_params=pltpu.CompilerParams(vmem_limit_bytes=56 * 2**20),
    )(x, vec24, vec72, wqkv)


def middle_kernel(
    len_ref, x_ref, o_ref, cot_ref, vec24_ref, vec96_ref, wout_all, wup_all, wdown_all,
    mixed_ref, do_ref, dy1_ref, gout_ref, gup_ref, gdown_ref, small24_ref, small96_ref,
    f_t, du, h2_t, dy, dz, o_t, wout_ref, wup_ref, wdown_ref, flat, load, store,
):
    step = pl.program_id(0)
    steps = pl.num_programs(0)
    rows_at = pl.multiple_of(step * MID, MID)
    here = pl.ds(rows_at, MID)
    chunk = 768
    weights = ((wout_all, wout_ref), (wup_all, wup_ref), (wdown_all, wdown_ref))
    loads = [pltpu.make_async_copy(a, b, load.at[i]) for i, (a, b) in enumerate(weights)]

    @pl.when(step == 0)
    def _():
        for copy in loads:
            copy.start()
        small24_ref[...] = jnp.zeros_like(small24_ref)
        small96_ref[...] = jnp.zeros_like(small96_ref)
        loads[0].wait()

    attended = o_ref[...]
    y1 = x_ref[...].astype(F32) + nn(attended, wout_ref[...]) + vec24_ref[2:3, :]
    normed, inverse = norm_parts(y1)
    h2 = (normed * vec24_ref[3:4, :] + vec24_ref[4:5, :]).astype(BF16)
    rows = lax.broadcasted_iota(jnp.int32, (MID, D), 0) + rows_at
    upstream = jnp.where(rows < len_ref[0], cot_ref[...].astype(F32), 0.0)
    upstream16 = upstream.astype(BF16)
    h2_t[:, here] = h2.T
    o_t[:, here] = attended.T
    dy[here, :] = upstream16
    small24_ref[5:6, :] += jnp.sum(upstream, axis=0, keepdims=True)

    @pl.when(step == 0)
    def _():
        loads[1].wait()
        loads[2].wait()

    y = y1 + vec24_ref[5:6, :]
    dh2 = None
    for c in range(FF // CHUNK):
        cols = slice(c * CHUNK, (c + 1) * CHUNK)
        u = nn(h2, wup_ref[:, cols]) + vec96_ref[7:8, cols]
        square = u * u
        t = jnp.tanh(u * (0.7978845608028654 + 0.035677408136300125 * square))
        half = 0.5 * (1.0 + t)
        f = (u * half).astype(BF16)
        slope = half + (0.5 * u) * (1.0 - t * t) * (
            0.7978845608028654 + 0.10703222440890037 * square
        )
        y = y + nn(f, wdown_ref[cols, :])
        df = nt(upstream16, wdown_ref[cols, :])
        d16 = (df * slope).astype(BF16)
        du[here, cols] = d16
        f_t[cols, here] = f.T
        small96_ref[7:8, cols] += jnp.sum(d16.astype(F32), axis=0, keepdims=True)
        part = nt(d16, wup_ref[:, cols])
        dh2 = part if c == 0 else dh2 + part
    mixed_ref[...] = y.astype(BF16)
    e = dh2 * vec24_ref[3:4, :]
    dy1 = dy[here, :].astype(F32) + norm_back(e, normed, inverse)
    dz16 = dy1.astype(BF16)
    dy1_ref[...] = dy1
    do_ref[...] = nt(dz16, wout_ref[...]).astype(BF16)
    small24_ref[2:3, :] += jnp.sum(dz16.astype(F32), axis=0, keepdims=True)
    small24_ref[3:4, :] += jnp.sum(dh2 * normed, axis=0, keepdims=True)
    small24_ref[4:5, :] += jnp.sum(dh2, axis=0, keepdims=True)
    dz[here, :] = dz16

    @pl.when(step == steps - 1)
    def _():
        shards = gout_ref.shape[0]

        def pipeline(count, stage, compute, target):
            def one(k, carry):
                slot = lax.rem(k, 2)
                copy = pltpu.make_async_copy(stage.at[slot], target(k), store.at[slot])

                @pl.when(k >= 2)
                def _():
                    copy.wait()

                stage[slot] = compute(k)
                copy.start()
                return carry

            lax.fori_loop(0, count, one, 0)
            for k in (count - 2, count - 1):
                pltpu.make_async_copy(stage.at[k % 2], target(k), store.at[k % 2]).wait()

        def blocks(value, depth):
            return value.reshape(value.shape[0] // depth, depth, value.shape[1]).astype(BF16)

        def block(k):
            return pl.ds(pl.multiple_of(k * chunk, chunk), chunk)

        pipeline(
            4,
            flat,
            lambda k: blocks(nn(f_t[block(k), :], dy[...]), D // shards),
            lambda k: gdown_ref.at[pl.ds(k * shards, shards)],
        )
        pipeline(
            4,
            flat,
            lambda k: blocks(nn(h2_t[...], du[:, block(k)]), D // shards),
            lambda k: gup_ref.at[:, :, block(k)],
        )
        flat[0] = blocks(nn(o_t[...], dz[...]), D // shards)
        last = pltpu.make_async_copy(flat.at[0], gout_ref, store.at[0])
        last.start()
        last.wait()


def middle_call(lengths, x, attended, cotangent, vec24, vec96, wout, wup, wdown, shards):
    length = x.shape[0]

    def rows(width):
        return pl.BlockSpec((MID, width), lambda i: (i, 0))

    def whole(shape):
        return pl.BlockSpec(shape, lambda i: (0,) * len(shape), pipeline_mode=pl.Buffered(1))

    anywhere = pl.BlockSpec(memory_space=pl.ANY)
    outs = (
        ((length, D), BF16, rows(D)),
        ((length, D), BF16, rows(D)),
        ((length, D), F32, rows(D)),
        ((shards, D // shards, D), BF16, anywhere),
        ((shards, D // shards, FF), BF16, anywhere),
        ((FF // D * shards, D // shards, D), BF16, anywhere),
        ((16, D), F32, whole((16, D))),
        ((16, FF), F32, whole((16, FF))),
    )
    return pl.pallas_call(
        middle_kernel,
        grid=(length // MID,),
        out_shape=tuple(jax.ShapeDtypeStruct(s, t) for s, t, _ in outs),
        in_specs=[
            pl.BlockSpec(memory_space=pltpu.SMEM),
            rows(D), rows(D), rows(D),
            whole(vec24.shape), whole(vec96.shape),
            anywhere, anywhere, anywhere,
        ],
        out_specs=tuple(b for _, _, b in outs),
        scratch_shapes=[
            VMEM((FF, length), BF16),
            VMEM((length, FF), BF16),
            VMEM((D, length), BF16),
            VMEM((length, D), BF16),
            VMEM((length, D), BF16),
            VMEM((D, length), BF16),
            VMEM(wout.shape, BF16),
            VMEM(wup.shape, BF16),
            VMEM(wdown.shape, BF16),
            VMEM((2, shards, D // shards, D), BF16),
            pltpu.SemaphoreType.DMA((3,)),
            pltpu.SemaphoreType.DMA((2,)),
        ],
        compiler_params=pltpu.CompilerParams(
            dimension_semantics=("arbitrary",), vmem_limit_bytes=63 * 2**20
        ),
    )(lengths, x, attended, cotangent, vec24, vec96, wout, wup, wdown)


def tail_rows(block, x_ref, dy1_ref, vec24_ref, wqkv_ref, dqkv_ref, h1_t, gx_ref, s24_ref, s72_ref):
    here = pl.ds(pl.multiple_of(block * BLK, BLK), BLK)
    normed, inverse = norm_parts(x_ref[here, :].astype(F32))
    if h1_t is not None:
        h1_t[:, here] = (normed * vec24_ref[0:1, :] + vec24_ref[1:2, :]).astype(BF16).T
    grad = dqkv_ref[here, :]
    dh1 = nt(grad, wqkv_ref[...])
    e = dh1 * vec24_ref[0:1, :]
    gx_ref[here, :] = (dy1_ref[here, :] + norm_back(e, normed, inverse)).astype(BF16)
    s24_ref[0:1, :] += jnp.sum(dh1 * normed, axis=0, keepdims=True)
    s24_ref[1:2, :] += jnp.sum(dh1, axis=0, keepdims=True)
    s72_ref[6:7, :] += jnp.sum(grad.astype(F32), axis=0, keepdims=True)


def backward_kernel(
    x_ref, dy1_ref, vec24_ref, wqkv_ref, qkv_ref, o_ref, do_ref, lse_ref,
    gx_ref, gqkv_ref, s24_ref, s72_ref,
    dqkv, h1_t, kt, dk, dv,
):
    s24_ref[...] = jnp.zeros_like(s24_ref)
    s72_ref[...] = jnp.zeros_like(s72_ref)
    lax.fori_loop(
        0,
        HEADS // 2,
        lambda p, c: (
            attention_back_pair(p, qkv_ref, o_ref, do_ref, lse_ref, dqkv, kt, dk, dv),
            c,
        )[1],
        0,
    )
    lax.fori_loop(
        0,
        x_ref.shape[0] // BLK,
        lambda b, c: (
            tail_rows(
                b, x_ref, dy1_ref, vec24_ref, wqkv_ref, dqkv, h1_t, gx_ref, s24_ref, s72_ref
            ),
            c,
        )[1],
        0,
    )
    shards = gqkv_ref.shape[0]
    many = shards // 4

    def one(i, carry):
        left = pl.ds(pl.multiple_of(i * (D // 4), D // 4), D // 4)
        for part in range(3):
            cols = slice(part * D, (part + 1) * D)
            value = nn(h1_t[left, :], dqkv[:, cols]).reshape(many, D // shards, D)
            gqkv_ref[pl.ds(i * many, many), :, cols] = value.astype(BF16)
        return carry

    lax.fori_loop(0, 4, one, 0)


def backward_call(x, dy1, vec24, wqkv, qkv, attended, grad_attended, lse, shards):
    length = x.shape[0]
    return pl.pallas_call(
        backward_kernel,
        out_shape=(
            jax.ShapeDtypeStruct((length, D), BF16),
            jax.ShapeDtypeStruct((shards, D // shards, 3 * D), BF16),
            jax.ShapeDtypeStruct((16, D), F32),
            jax.ShapeDtypeStruct((16, 3 * D), F32),
        ),
        in_specs=[pl.BlockSpec(memory_space=VMEM)] * 8,
        out_specs=(pl.BlockSpec(memory_space=VMEM),) * 4,
        scratch_shapes=[
            VMEM((length, 3 * D), BF16),
            VMEM((D, length), BF16),
            VMEM((128, length), BF16),
            VMEM((length, 128), F32),
            VMEM((length, 128), F32),
        ],
        compiler_params=pltpu.CompilerParams(vmem_limit_bytes=60 * 2**20),
    )(x, dy1, vec24, wqkv, qkv, attended, grad_attended, lse)


def place():
    wide = lax.axis_index("wide")
    return wide // 4, (wide // 2) % 2, wide % 2, lax.axis_index("narrow")


def device(z, x, c, y):
    return ((z * 2 + x) * 2 + c, y)


def greet():
    z, x, c, y = place()
    barrier = pltpu.get_barrier_semaphore()
    peers = [device(lax.rem(z + d, 4), x, c, y) for d in (1, 2, 3)]
    peers += [device(z, 1 - x, c, y), device(z, x, c, 1 - y), device(z, x, 1 - c, y)]
    for peer in peers:
        pl.semaphore_signal(barrier, inc=1, device_id=peer, device_id_type=MESH)
    pl.semaphore_wait(barrier, len(peers))


def remote(src, dst, sems, slot, peer):
    return pltpu.make_async_remote_copy(
        src_ref=src, dst_ref=dst, send_sem=sems[0].at[slot], recv_sem=sems[1].at[slot],
        device_id=peer, device_id_type=MESH,
    )


FIRST_Z = (("z", "x", "y"), ("z", "y", "x"))
LATER_Z = (("x", "z", "y"), ("y", "z", "x"))
UP_ORDERS = FIRST_Z
DOWN_ORDERS = LATER_Z


def peers_of(z, x, c, y):
    return {
        "z": [device(lax.rem(z + d, 4), x, c, y) for d in (1, 2, 3)],
        "x": [device(z, 1 - x, c, y)],
        "y": [device(z, x, c, 1 - y)],
        "c": [device(z, x, 1 - c, y)],
    }


def halves(low, high):
    cut = (high - low) // 256 * 128
    return [(low, low + cut), (low + cut, high)] if cut else [(low, high)]


def window(span):
    return pl.ds(span[0], span[1] - span[0])


class Gather:
    slots = 16

    def __init__(self, own, full, sems, local, rows=None, cols=None, orders=FIRST_Z):
        height, width = full.shape[-2:]
        span = cols or (0, width)
        rows = slice(None) if rows is None else window(rows)
        z, x, c, y = place()
        here = {"z": z, "x": x, "y": y}
        peers = peers_of(z, x, c, y)
        lanes = list(zip(halves(*span), orders))
        self.groups = [[], [], []]
        self.core = [[], [], [], []]
        slot = 0

        def at(state, cols):
            return full.at[state["z"], state["x"], c, state["y"], rows, window(cols)]

        for k in range(3):
            items = lanes
            if k == 0 and all(order[0] == orders[0][0] for _, order in lanes):
                items = [(span, orders[0])]
            for cols, order in items:
                now = {d: slice(None) if d in order[:k] else here[d] for d in "zxy"}
                source = own.at[rows, window(cols)] if k == 0 else at(now, cols)
                for peer in peers[order[k]]:
                    self.groups[k].append(remote(source, at(now, cols), sems, slot, peer))
                    slot += 1
                if "z" in order[: k + 1]:
                    later = dict(now)
                    later[order[k]] = slice(None) if order[k] == "z" else 1 - here[order[k]]
                    view = at(later, cols)
                    self.core[k + 1].append(remote(view, view, sems, slot, peers["c"][0]))
                    slot += 1
        self.kept = pltpu.make_async_copy(own.at[rows, window(span)], at(here, span), local)

    def run(self, stage):
        if stage == 0:
            self.kept.start()
        elif stage == 1:
            self.kept.wait()
        if 1 <= stage <= 3:
            for copy in self.groups[stage - 1]:
                copy.wait_recv()
        if stage <= 2:
            for copy in self.groups[stage]:
                copy.start()
        if stage <= 3:
            for copy in self.core[stage]:
                copy.start()
        every_core = [copy for copies in self.core for copy in copies]
        if stage == 4:
            for copy in every_core:
                copy.wait_recv()
        if stage == 5:
            for copy in every_core + [copy for copies in self.groups for copy in copies]:
                copy.wait_send()


def spread(blocks, each):
    width = 32 * each
    lane = lax.broadcasted_iota(jnp.int32, (128, width), 0)
    col = lax.broadcasted_iota(jnp.int32, (128, width), 1)
    value = nn(blocks, (lax.rem(col, each) == lane).astype(BF16)).reshape(32, 16, width)
    shard = lax.broadcasted_iota(jnp.int32, (32, 16, width), 0)
    col = lax.broadcasted_iota(jnp.int32, (32, 16, width), 2)
    inside = (col >= shard * each) & (col < shard * each + each)
    return jnp.sum(jnp.where(inside, value, 0.0), axis=0)


FORWARD = {
    "n": ("X0", "S0", "Y0",),
    "h": ("Z0", "X1", "S1", "O0", "X2", "U0", "S2", "Y1", "D0", "X3", "S3", "S4", "Y2",),
    0: ("X4", "Z1", "V0", "O1", "E0",),
    1: ("Y3", "Z2",),
    3: ("O2",),
    5: ("Z3", "U1", "D1",),
    8: ("O3",),
    9: ("V1",),
    10: ("Y4", "U2",),
    14: ("V2", "E1",),
    15: ("U3",),
    20: ("Z4", "D2",),
    21: ("V3",),
    24: ("E2",),
    25: ("D3",),
    "last": ("E3", "O4", "U4", "D4", "V4", "E4",),
}


def runner(parts, table):
    def run(at):
        for word in table.get(at, ()):
            parts[word[0]].run(int(word[1]))

    return run


def when_run(run, table, value, positions):
    for number, at in positions:
        if at in table:

            @pl.when(value == number)
            def _():
                run(at)


def gather_forward_kernel(
    x_ref, small_ref, wqkv_own, wout_own, wup_own, wdown_own,
    wqkv_out, wout_full, wup_full, wdown_full, vec24_ref, vec96_ref, qkv_out, o_out, lse_ref,
    small_full, wqkv_full, vec72, own_groups, hidden, vt, wqkv_ref, qkv_ref, o_ref,
    send, recv, local, store,
):
    greet()
    results = ((wqkv_ref, wqkv_out), (qkv_ref, qkv_out), (o_ref, o_out))
    stores = [pltpu.make_async_copy(a, b, store.at[i]) for i, (a, b) in enumerate(results)]
    length = x_ref.shape[0]
    steps = length // BLK
    half = wdown_full.shape[-2] // 2
    parts = {}

    def add_part(name, own, full, **view):
        i = len(parts)
        parts[name] = Gather(own, full, (send.at[i], recv.at[i]), local.at[i], **view)

    add_part("S", small_ref, small_full)
    for group, name in enumerate("XYZ"):
        add_part(name, own_groups, wqkv_full, cols=(group * D, (group + 1) * D))
        for part in range(3):
            own_groups[:, (3 * group + part) * 256 : (3 * group + part + 1) * 256] = wqkv_own[
                :, part * D + group * 256 : part * D + (group + 1) * 256
            ]
    add_part("O", wout_own, wout_full)
    add_part("U", wup_own, wup_full, cols=(0, FF // 2), orders=UP_ORDERS)
    add_part("V", wup_own, wup_full, cols=(FF // 2, FF), orders=UP_ORDERS)
    add_part("D", wdown_own, wdown_full, rows=(0, half), orders=DOWN_ORDERS)
    add_part("E", wdown_own, wdown_full, rows=(half, 2 * half), orders=DOWN_ORDERS)
    run = runner(parts, FORWARD)
    run("n")

    def normalize(block, carry):
        here = pl.ds(pl.multiple_of(block * BLK, BLK), BLK)
        normed, _ = norm_parts(x_ref[here, :].astype(F32))
        hidden[here, :] = (normed * vec24_ref[0:1, :] + vec24_ref[1:2, :]).astype(BF16)
        return carry

    run("h")
    blocks = small_full[...].reshape(32 * 16, 128)
    for ref, each in zip((vec24_ref, vec72, vec96_ref), (24, 72, 96)):
        ref[...] = spread(blocks, each)
    lax.fori_loop(0, steps, normalize, 0)

    def group_qkv(group):
        wide = pl.ds(pl.multiple_of(group * D, D), D)

        def spot(part):
            return pl.ds(pl.multiple_of(part * D + group * 256, 256), 256)

        def flatten(i, carry):
            two = wqkv_full[i // 4, (i // 2) % 2, i % 2, :, :, wide].astype(F32)
            two = two.reshape(D // 16, D).astype(BF16)
            rows = pl.ds(pl.multiple_of(i * (D // 16), D // 16), D // 16)
            for part in range(3):
                wqkv_ref[rows, spot(part)] = two[:, part * 256 : (part + 1) * 256]
            return carry

        lax.fori_loop(0, 16, flatten, 0)

        def rows_qkv(block, carry):
            here = pl.ds(pl.multiple_of(block * BLK, BLK), BLK)
            for part in range(3):
                value = nn(hidden[here, :], wqkv_ref[:, spot(part)]) + vec72[6:7, spot(part)]
                qkv_ref[here, spot(part)] = value.astype(BF16)
            return carry

        lax.fori_loop(0, steps, rows_qkv, 0)

    def one(pair, carry):
        def event(j):
            spots = [(p, p * (steps + 1) + 1 + j) for p in range(HEADS // 2)]
            when_run(run, FORWARD, pair, spots)

        event(-1)

        @pl.when(pair % 2 == 0)
        def _():
            group_qkv(pair // 2)

        attention_pair(pair, qkv_ref, o_ref, lse_ref, vt, event)
        return carry

    lax.fori_loop(0, HEADS // 2, one, 0)
    for copy in stores:
        copy.start()
    run("last")
    for part in parts.values():
        part.run(5)
    for copy in stores:
        copy.wait()


def gather_forward_call(x, small, wqkv, wout, wup, wdown):
    length = x.shape[0]
    anywhere = pl.BlockSpec(memory_space=pl.ANY)
    inside = pl.BlockSpec(memory_space=VMEM)

    def full(own):
        return jax.ShapeDtypeStruct((4, 2, 2, 2, *own.shape), BF16)

    return pl.pallas_call(
        gather_forward_kernel,
        out_shape=(
            jax.ShapeDtypeStruct((D, 3 * D), BF16),
            full(wout), full(wup), full(wdown),
            jax.ShapeDtypeStruct((16, D), F32),
            jax.ShapeDtypeStruct((16, FF), F32),
            jax.ShapeDtypeStruct((length, 3 * D), BF16),
            jax.ShapeDtypeStruct((length, D), BF16),
            jax.ShapeDtypeStruct((HEADS // 2, 8, length), F32),
        ),
        in_specs=[inside] * 3 + [anywhere] * 3,
        out_specs=(*[anywhere] * 4, inside, inside, anywhere, anywhere, inside),
        scratch_shapes=[
            VMEM((4, 2, 2, 2, 16, 128), BF16),
            VMEM((4, 2, 2, 2, *wqkv.shape), BF16),
            VMEM((16, 3 * D), F32),
            VMEM(wqkv.shape, BF16),
            VMEM((length, D), BF16),
            VMEM((128, length), BF16),
            VMEM((D, 3 * D), BF16),
            VMEM((length, 3 * D), BF16),
            VMEM((length, D), BF16),
            pltpu.SemaphoreType.DMA((9, Gather.slots)),
            pltpu.SemaphoreType.DMA((9, Gather.slots)),
            pltpu.SemaphoreType.DMA((9,)),
            pltpu.SemaphoreType.DMA((3,)),
        ],
        compiler_params=pltpu.CompilerParams(
            collective_id=1, has_side_effects=True, vmem_limit_bytes=60 * 2**20
        ),
    )(x, small, wqkv, wout, wup, wdown)


SIZES = {"z": 4, "x": 2, "y": 2}


def held_after(order, k):
    return [d for d in "zxy" if d not in order[:k]]


class Scatter:
    slots = 12

    def __init__(self, grads, buffers, sems, local, put, rows=None, cols=None, orders=FIRST_Z):
        height, width = grads.shape[-2:]
        low, high = cols or (0, width)
        rows = slice(None) if rows is None else window(rows)
        cols = slice(None) if cols is None else window(cols)
        z, x, c, y = place()
        self.here = {"z": z, "x": x, "y": y}
        self.core_at = c
        peers = peers_of(z, x, c, y)
        self.grads, self.put = grads, put
        self.mine, self.one, *rest = buffers
        if self.mine is not None:
            self.kept = pltpu.make_async_copy(grads.at[:, :, c, :, rows, cols], self.mine, local)
        self.groups = [[remote(grads.at[:, :, 1 - c, :, rows, cols], self.one, sems, 0, peers["c"][0])]]
        self.groups += [[], [], []]
        self.lanes = []
        slot = 1
        for span, order in zip(halves(0, high - low), orders):
            order = order[::-1]
            got = [rest.pop(0) for _ in range(3)]
            self.lanes.append((window(span), order, got))
            for k in range(3):
                source = self.one if k == 0 else got[k - 1]
                cut = (slice(None), window(span)) if k == 0 else (slice(None), slice(None))
                if k > 0 and order[k - 1] == "z":
                    source = source.at[0]
                if order[k] == "z":
                    others = [lax.rem(z + d, 4) for d in (1, 2, 3)]
                else:
                    others = [1 - self.here[order[k]]]
                for i, (other, peer) in enumerate(zip(others, peers[order[k]])):
                    index = [other if d == order[k] else slice(None) for d in held_after(order, k)]
                    target = got[k].at[i] if order[k] == "z" else got[k]
                    self.groups[k + 1].append(
                        remote(source.at[(*index, *cut)], target, sems, slot, peer)
                    )
                    slot += 1

    @staticmethod
    def shapes(r, n, mine, orders=FIRST_Z):
        result = [VMEM((4, 2, 2, r, n), BF16)] * (2 if mine else 1)
        for (low, high), order in zip(halves(0, n), orders):
            order = order[::-1]
            for k in range(3):
                held = [SIZES[d] for d in held_after(order, k + 1)]
                lead = [3] if order[k] == "z" else []
                result.append(VMEM((*lead, *held, r, high - low), BF16))
        return result

    def add(self, lane, k):
        cols, order, got = lane
        before = held_after(order, k)
        after = held_after(order, k + 1)

        def total(index):
            at = dict(zip(after, index))
            at[order[k]] = self.here[order[k]]
            where = tuple(at[d] for d in before)
            if k == 0:
                value = self.one[(*where, slice(None), cols)]
            else:
                lead = (0,) if order[k - 1] == "z" else ()
                value = got[k - 1][(*lead, *where)]
            lead = [(i,) for i in range(3)] if order[k] == "z" else [()]
            if k == 2:
                value = value.astype(F32)
                for i in lead:
                    value = value + got[k][i + index].astype(F32)
                return value
            for i in lead:
                value = value + got[k][i + index]
            got[k][lead[0] + index] = value

        if not after:
            return total(())
        sizes = [SIZES[d] for d in after]

        def loop(i, carry):
            if len(sizes) == 1:
                total((i,))
            else:
                for j in range(sizes[1]):
                    total((i, j))
            return carry

        lax.fori_loop(0, sizes[0], loop, 0)

    def run(self, stage):
        if stage == 0 and self.mine is not None:
            self.kept.start()
        if stage == 1 and self.mine is not None:
            self.kept.wait()
        if 1 <= stage <= 4:
            for copy in self.groups[stage - 1]:
                copy.wait_recv()
        if stage == 1:

            def add(i, carry):
                a, b = i // 2, i % 2
                own = self.grads[a, b, self.core_at] if self.mine is None else self.mine[a, b]
                self.one[a, b] = self.one[a, b] + own
                return carry

            lax.fori_loop(0, 8, add, 0)
        if stage in (2, 3):
            for lane in self.lanes:
                self.add(lane, stage - 2)
        if stage == 4:
            values = [self.add(lane, 2) for lane in self.lanes]
            self.put(values[0] if len(values) == 1 else jnp.concatenate(values, axis=1))
        if stage <= 3:
            for copy in self.groups[stage]:
                copy.start()
        if stage == 5:
            for copies in self.groups:
                for copy in copies:
                    copy.wait_send()


def fold(values, each, row):
    width = 32 * each
    shard = lax.broadcasted_iota(jnp.int32, (32, 16, width), 0)
    col = lax.broadcasted_iota(jnp.int32, (32, 16, width), 2)
    inside = (col >= shard * each) & (col < shard * each + each)
    spreaded = jnp.where(inside, values[None], 0.0).reshape(32 * 16, width).astype(BF16)
    lane = lax.broadcasted_iota(jnp.int32, (128, width), 0)
    col = lax.broadcasted_iota(jnp.int32, (128, width), 1)
    return nt(spreaded, (lax.rem(col, each) == lane).astype(BF16))


BACKWARD = {
    "h": ("D0", "E0", "U0",),
    0: ("V0", "O0",),
    1: ("D1",),
    5: ("E1",),
    6: ("D2",),
    "g0": ("X0", "U1",),
    10: ("V1",),
    12: ("E2",),
    14: ("D3", "U2",),
    "g1": ("V2", "Y0",),
    17: ("O1", "U3",),
    18: ("X1",),
    20: ("E3",),
    21: ("V3", "O2", "X2",),
    22: ("Y1",),
    23: ("O3",),
    "t0": ("Z0",),
    "t1": ("X3", "Y2", "Z1",),
    "t3": ("Y3",),
    "f": ("Z2",),
    "e": ("S0",),
    "last": ("S1", "Z3", "S2", "S3", "D4", "E4", "U4", "V4", "O4", "X4", "Y4", "Z4", "S4",),
}
GROUPS = 3


def scatter_backward_kernel(
    x_all, dy1_all, vec24_ref, wqkv_all, qkv_all, o_all, do_all, lse_ref, s24_mid, s96_mid,
    gout_all, gup_all, gdown_all,
    gx_ref, gqkv_ref, gout_ref, gup_ref, gdown_ref, small_ref,
    dqkv, h1_t, kt, dk, dv, s24_ref, s72_ref, small_all,
    x_ref, qkv_ref, do_ref, o_ref, dy1_ref, wqkv_ref, *buffers,
):
    send, recv, local, load = buffers[-4:]
    buffers = list(buffers[:-4])
    greet()
    inputs = (
        (x_all, x_ref), (qkv_all, qkv_ref), (do_all, do_ref), (o_all, o_ref), (dy1_all, dy1_ref),
        (wqkv_all, wqkv_ref),
    )
    loads = [pltpu.make_async_copy(a, b, load.at[i]) for i, (a, b) in enumerate(inputs)]
    half = gdown_all.shape[-2] // 2
    parts = {}

    def add_part(name, grads, mine, put, **view):
        i = len(parts)
        held = [buffers.pop(0)] if mine else [None]
        count = 4 if len(halves(0, grads.shape[-1])) == 1 else 7
        held += [buffers.pop(0) for _ in range(count)]
        parts[name] = Scatter(grads, held, (send.at[i], recv.at[i]), local.at[i], put, **view)

    def put_at(ref, rows, cols):
        def put(value):
            ref[rows, cols] = value

        return put

    every = slice(None)
    for name, k in (("U", 0), ("V", 1)):
        cols = (k * FF // 2, (k + 1) * FF // 2)
        add_part(name, gup_all, True, put_at(gup_ref, every, slice(*cols)), cols=cols, orders=UP_ORDERS)
    for name, k in (("D", 0), ("E", 1)):
        rows = (k * half, (k + 1) * half)
        add_part(name, gdown_all, True, put_at(gdown_ref, slice(*rows), every), rows=rows, orders=DOWN_ORDERS)
    add_part("O", gout_all, True, put_at(gout_ref, every, every))
    groups = [buffers.pop(0) for _ in range(GROUPS)]

    def put_group(group):
        def put(value):
            for part in range(3):
                low = part * D + group * 256
                gqkv_ref[:, low : low + 256] = value[:, part * 256 : (part + 1) * 256]

        return put

    for group, name in enumerate("XYZ"):
        add_part(name, groups[group], False, put_group(group))
    add_part("S", small_all, False, put_at(small_ref, every, every))

    run = runner(parts, BACKWARD)
    run("h")
    for copy in loads:
        copy.start()
    s24_ref[...] = jnp.zeros_like(s24_ref)
    s72_ref[...] = jnp.zeros_like(s72_ref)
    length = x_ref.shape[0]
    steps = length // BLK

    def hidden_rows(block, carry):
        here = pl.ds(pl.multiple_of(block * BLK, BLK), BLK)
        normed, _ = norm_parts(x_ref[here, :].astype(F32))
        hidden = (normed * vec24_ref[0:1, :] + vec24_ref[1:2, :]).astype(BF16)
        h1_t[:, here] = hidden.T
        return carry

    loads[0].wait()
    lax.fori_loop(0, steps, hidden_rows, 0)
    for copy in loads[1:4]:
        copy.wait()

    def group_grads(group):
        def one(i, carry):
            left = pl.ds(pl.multiple_of(i * (D // 4), D // 4), D // 4)
            for part in range(3):
                low = part * D + group * 256
                value = nn(h1_t[left, :], dqkv[:, low : low + 256])
                value = value.reshape(2, 2, 2, D // 32, 256).astype(BF16)
                groups[group][i, :, :, :, :, part * 256 : (part + 1) * 256] = value
            return carry

        lax.fori_loop(0, 4, one, 0)

    def one(pair, carry):
        def event(j):
            at_step = steps - 1 - j
            if at_step == 0:
                for group in range(GROUPS - 1):

                    @pl.when(pair == 2 * group + 2)
                    def _():
                        group_grads(group)
                        run(f"g{group}")

            spots = [(p, p * steps + at_step) for p in range(HEADS // 2)]
            when_run(run, BACKWARD, pair, spots)

        attention_back_pair(pair, qkv_ref, o_ref, do_ref, lse_ref, dqkv, kt, dk, dv, event)
        return carry

    lax.fori_loop(0, HEADS // 2, one, 0)
    run("g2")
    group_grads(GROUPS - 1)
    for copy in loads[4:]:
        copy.wait()

    def tail(block, carry):
        when_run(run, BACKWARD, block, [(b, f"t{b}") for b in range(steps)])
        tail_rows(block, x_ref, dy1_ref, vec24_ref, wqkv_ref, dqkv, None, gx_ref, s24_ref, s72_ref)
        return carry

    lax.fori_loop(0, steps, tail, 0)
    run("f")
    total = fold(s24_ref[...] + s24_mid[...], 24, 0)
    total = total + fold(s72_ref[...], 72, 6) + fold(s96_mid[...], 96, 7)
    small_all[...] = total.reshape(4, 2, 2, 2, 16, 128).astype(BF16)
    run("e")
    run("last")
    for part in parts.values():
        part.run(5)


def scatter_backward_call(
    x, dy1, vec24, wqkv, qkv, attended, grad_attended, lse, s24, s96, gout, gup, gdown
):
    length = x.shape[0]
    anywhere = pl.BlockSpec(memory_space=pl.ANY)
    inside = pl.BlockSpec(memory_space=VMEM)
    deep = gdown.shape[-2]
    scratch = [
        VMEM((length, 3 * D), BF16),
        VMEM((D, length), BF16),
        VMEM((128, length), BF16),
        VMEM((length, 128), F32),
        VMEM((length, 128), F32),
        VMEM((16, D), F32),
        VMEM((16, 3 * D), F32),
        VMEM((4, 2, 2, 2, 16, 128), BF16),
        VMEM((length, D), BF16),
        VMEM((length, 3 * D), BF16),
        VMEM((length, D), BF16),
        VMEM((length, D), BF16),
        VMEM((length, D), F32),
        VMEM((D, 3 * D), BF16),
    ]
    for _ in range(2):
        scratch += Scatter.shapes(D // 32, FF // 2, True, UP_ORDERS)
    for _ in range(2):
        scratch += Scatter.shapes(deep // 2, D, True, DOWN_ORDERS)
    scratch += Scatter.shapes(D // 32, D, True)
    scratch += [VMEM((4, 2, 2, 2, D // 32, D), BF16)] * GROUPS
    for _ in range(GROUPS):
        scratch += Scatter.shapes(D // 32, D, False)
    scratch += Scatter.shapes(16, 128, False)
    scratch += [pltpu.SemaphoreType.DMA((9, Scatter.slots))] * 2 + [pltpu.SemaphoreType.DMA((9,))]
    scratch += [pltpu.SemaphoreType.DMA((6,))]
    return pl.pallas_call(
        scatter_backward_kernel,
        out_shape=(
            jax.ShapeDtypeStruct((length, D), BF16),
            jax.ShapeDtypeStruct((D // 32, 3 * D), F32),
            jax.ShapeDtypeStruct((D // 32, D), F32),
            jax.ShapeDtypeStruct((D // 32, FF), F32),
            jax.ShapeDtypeStruct((deep, D), F32),
            jax.ShapeDtypeStruct((16, 128), F32),
        ),
        in_specs=[
            anywhere, anywhere, inside, *[anywhere] * 4, inside, inside, inside, *[anywhere] * 3
        ],
        out_specs=(inside,) * 6,
        scratch_shapes=scratch,
        compiler_params=pltpu.CompilerParams(
            collective_id=2, has_side_effects=True, vmem_limit_bytes=63 * 2**20
        ),
    )(x, dy1, vec24, wqkv, qkv, attended, grad_attended, lse, s24, s96, gout, gup, gdown)


def shards(
    tokens, cotangent, lengths, ln1_gain, ln1_shift, qkv_weight, qkv_bias, out_weight, out_bias,
    ln2_gain, ln2_shift, up_weight, up_bias, down_weight, down_bias, *, special,
):
    vectors = (ln1_gain, ln1_shift, out_bias, ln2_gain, ln2_shift, down_bias, qkv_bias, up_bias)
    if special:
        small = jnp.stack(
            [jnp.pad(v, (0, 128 - v.shape[0])) for v in vectors] + [jnp.zeros((128,), BF16)] * 8
        )
        wqkv, wout, wup, wdown, vec24, vec96, qkv, attended, lse = gather_forward_call(
            tokens, small, qkv_weight, out_weight, up_weight, down_weight
        )
        wout, wup = (w.reshape(D, w.shape[-1]) for w in (wout, wup))
        wdown = wdown.reshape(FF, D)
    else:
        gather = functools.partial(lax.all_gather, axis_name=AXES, axis=0, tiled=True)
        wqkv, wout, wup, wdown = map(gather, (qkv_weight, out_weight, up_weight, down_weight))
        whole = [gather(v).astype(F32) for v in vectors]
        vec24 = jnp.pad(jnp.stack(whole[:6]), ((0, 10), (0, 0)))
        vec72 = jnp.pad(whole[6][None], ((6, 9), (0, 0)))
        vec96 = jnp.pad(whole[7][None], ((7, 8), (0, 0)))
        qkv, attended, lse = forward_call(tokens, vec24, vec72, wqkv)
    mixed, do, dy1, gout, gup, gdown, s24_mid, s96 = middle_call(
        lengths, tokens, attended, cotangent, vec24, vec96, wout, wup, wdown, 32
    )
    if special:
        gout, gup = (g.reshape(4, 2, 2, 2, *g.shape[1:]) for g in (gout, gup))
        gdown = gdown.reshape(4, 2, 2, 2, FF // 32, D)
        gx, gqkv, gout, gup, gdown, small = scatter_backward_call(
            tokens, dy1, vec24, wqkv, qkv, attended, do, lse, s24_mid, s96, gout, gup, gdown
        )
        sizes = [v.shape[0] for v in vectors]
        folded = [small[i, :n] for i, n in enumerate(sizes)]
    else:
        gx, gqkv, s24, s72 = backward_call(tokens, dy1, vec24, wqkv, qkv, attended, do, lse, 32)
        scatter = functools.partial(
            lax.psum_scatter, axis_name=AXES, scatter_dimension=0, tiled=True
        )
        gqkv, gout, gup = (scatter(g.reshape(D, -1).astype(F32)) for g in (gqkv, gout, gup))
        gdown = scatter(gdown.reshape(FF, D).astype(F32))
        both = s24 + s24_mid
        folded = [scatter(both[i]) for i in range(6)] + [scatter(s72[6]), scatter(s96[7])]
    return (
        mixed, gx, folded[0], folded[1], gqkv, folded[6], gout, folded[2], folded[3], folded[4],
        gup, folded[7], gdown, folded[5],
    )


def solution(mesh):
    flat, rows = P(AXES), P(AXES, None)
    in_specs = (
        rows, rows, flat, flat, flat, rows, flat, rows, flat, flat, flat, rows, flat, rows, flat,
    )
    out_specs = (
        rows, rows, flat, flat, rows, flat, rows, flat, flat, flat, rows, flat, rows, flat,
    )
    special = dict(mesh.shape) == {"wide": 16, "narrow": 2}
    return jax.shard_map(
        functools.partial(shards, special=special),
        mesh=mesh, in_specs=in_specs, out_specs=out_specs, check_vma=False,
    )
```

```python
import functools

import jax
import jax.numpy as jnp
from jax import lax
from jax.experimental import pallas as pl
from jax.experimental.pallas import tpu as pltpu
from jax.sharding import PartitionSpec as P

D = 768
FF = 3072
HEADS = 12
HEAD = 64
BLK = 256
MID = 256
CHUNK = 768
AXES = ("wide", "narrow")
MESH = pl.DeviceIdType.MESH
VMEM = pltpu.VMEM
F32 = jnp.float32
BF16 = jnp.bfloat16


def nn(left, right):
    return lax.dot_general(left, right, (((1,), (0,)), ((), ())), preferred_element_type=F32)


def nt(left, right):
    return lax.dot_general(left, right, (((1,), (1,)), ((), ())), preferred_element_type=F32)


def norm_parts(values):
    average = jnp.mean(values, axis=-1, keepdims=True)
    centered = values - average
    inverse = lax.rsqrt(jnp.mean(centered * centered, axis=-1, keepdims=True) + 1e-05)
    return centered * inverse, inverse


def norm_back(grad_normed, normed, inverse):
    first_mean = jnp.mean(grad_normed, axis=-1, keepdims=True)
    second_mean = jnp.mean(grad_normed * normed, axis=-1, keepdims=True)
    return inverse * (grad_normed - first_mean - normed * second_mean)


def lane_half(values, half):
    lanes = lax.broadcasted_iota(jnp.int32, values.shape, 1)
    keep = (lanes < HEAD) if half == 0 else (lanes >= HEAD)
    return jnp.where(keep, values, jnp.zeros_like(values))


def diagonal_keep():
    keys = lax.broadcasted_iota(jnp.int32, (BLK, BLK), 0)
    queries = lax.broadcasted_iota(jnp.int32, (BLK, BLK), 1)
    return keys <= queries


def column(pair, part):
    return pl.ds(pl.multiple_of(part * D + pair * 128, 128), 128)


def qkv_rows(block, x_ref, vec24_ref, vec72_ref, wqkv_ref, qkv_ref):
    rows = pl.ds(pl.multiple_of(block * BLK, BLK), BLK)
    normed, _ = norm_parts(x_ref[rows, :].astype(F32))
    hidden = (normed * vec24_ref[0:1, :] + vec24_ref[1:2, :]).astype(BF16)
    for part in range(3):
        cols = slice(part * D, (part + 1) * D)
        qkv_ref[rows, cols] = (nn(hidden, wqkv_ref[:, cols]) + vec72_ref[6:7, cols]).astype(BF16)


def attention_pair(pair, qkv_ref, o_ref, lse_ref, vt, event=lambda j: None):
    length = qkv_ref.shape[0]
    vt[...] = qkv_ref[:, column(pair, 2)].T
    keep = diagonal_keep()
    for j in range(length // BLK):
        event(j)
        span = (j + 1) * BLK
        rows = slice(j * BLK, span)
        query = qkv_ref[rows, column(pair, 0)] * jnp.asarray(0.125, BF16)
        keys = qkv_ref[0:span, column(pair, 1)]
        outs = []
        for half in range(2):
            s = nt(keys, lane_half(query, half))
            w = s * s + 1.0
            m = w * lax.rsqrt(w)
            tail = jnp.where(keep, m[j * BLK :], -1e30)
            m = tail if j == 0 else jnp.concatenate([m[: j * BLK], tail], axis=0)
            top = jnp.max(m, axis=0, keepdims=True)
            e = jnp.exp(m - top)
            total = jnp.sum(e, axis=0, keepdims=True)
            a = (jnp.tanh(s) * e).astype(BF16)
            outs.append(nn(vt[half * HEAD : (half + 1) * HEAD, 0:span], a) / total)
            lse_ref[pair, half : half + 1, rows] = top + jnp.log(total)
        o_ref[rows, column(pair, 0)] = jnp.concatenate(outs, axis=0).T.astype(BF16)


def attention_back_pair(
    pair, qkv_ref, o_ref, do_ref, lse_ref, dqkv_ref, kt, dk, dv, event=lambda j: None
):
    length = qkv_ref.shape[0]
    kt[...] = qkv_ref[:, column(pair, 1)].T
    keep = diagonal_keep()
    lanes = lax.broadcasted_iota(jnp.int32, (8, 128), 1)
    sublanes = lax.broadcasted_iota(jnp.int32, (8, 128), 0)
    pick = (lanes // HEAD == sublanes).astype(F32)
    steps = length // BLK
    for j in reversed(range(steps)):
        event(j)
        span = (j + 1) * BLK
        rows = slice(j * BLK, span)
        query = qkv_ref[rows, column(pair, 0)] * jnp.asarray(0.125, BF16)
        grad = do_ref[rows, column(pair, 0)]
        product = grad.astype(F32) * o_ref[rows, column(pair, 0)].astype(F32)
        inner = lax.dot_general(
            pick, product, (((1,), (1,)), ((), ())),
            precision=lax.Precision.HIGHEST, preferred_element_type=F32,
        )
        keys = qkv_ref[0:span, column(pair, 1)]
        values = qkv_ref[0:span, column(pair, 2)]
        dqs = []
        dks = None
        dvs = None
        for half in range(2):
            query_half = lane_half(query, half)
            grad_half = lane_half(grad, half)
            s = nt(keys, query_half)
            da = nt(values, grad_half)
            w = s * s + 1.0
            r = lax.rsqrt(w)
            p = jnp.exp(w * r - lse_ref[pair, half : half + 1, rows])
            tail = jnp.where(keep, p[j * BLK :], 0.0)
            p = tail if j == 0 else jnp.concatenate([p[: j * BLK], tail], axis=0)
            t = jnp.tanh(s)
            a = (t * p).astype(BF16)
            ds = p * (da * (1.0 - t * t) + (da * t - inner[half : half + 1, :]) * (s * r))
            ds = ds.astype(BF16)
            dqs.append(nn(kt[half * HEAD : (half + 1) * HEAD, 0:span], ds))
            this_dk = nn(ds, query_half)
            this_dv = nn(a, grad_half)
            dks = this_dk if half == 0 else dks + this_dk
            dvs = this_dv if half == 0 else dvs + this_dv
        dqkv_ref[rows, column(pair, 0)] = (jnp.concatenate(dqs, axis=0).T * 0.125).astype(BF16)
        if j == steps - 1:
            dk[...] = dks
            dv[...] = dvs
        else:
            dk[0:span, :] += dks
            dv[0:span, :] += dvs
    dqkv_ref[:, column(pair, 1)] = dk[...].astype(BF16)
    dqkv_ref[:, column(pair, 2)] = dv[...].astype(BF16)


def forward_kernel(x_ref, vec24_ref, vec72_ref, wqkv_ref, qkv_ref, o_ref, lse_ref, vt):
    lax.fori_loop(
        0,
        x_ref.shape[0] // BLK,
        lambda b, c: (qkv_rows(b, x_ref, vec24_ref, vec72_ref, wqkv_ref, qkv_ref), c)[1],
        0,
    )
    lax.fori_loop(
        0, HEADS // 2, lambda p, c: (attention_pair(p, qkv_ref, o_ref, lse_ref, vt), c)[1], 0
    )


def forward_call(x, vec24, vec72, wqkv):
    length = x.shape[0]
    return pl.pallas_call(
        forward_kernel,
        out_shape=(
            jax.ShapeDtypeStruct((length, 3 * D), BF16),
            jax.ShapeDtypeStruct((length, D), BF16),
            jax.ShapeDtypeStruct((HEADS // 2, 8, length), F32),
        ),
        in_specs=[pl.BlockSpec(memory_space=VMEM)] * 4,
        out_specs=(pl.BlockSpec(memory_space=VMEM),) * 3,
        scratch_shapes=[VMEM((128, length), BF16)],
        compiler_params=pltpu.CompilerParams(vmem_limit_bytes=56 * 2**20),
    )(x, vec24, vec72, wqkv)


def middle_kernel(
    len_ref, x_ref, o_ref, cot_ref, vec24_ref, vec96_ref, wout_all, wup_all, wdown_all,
    mixed_ref, do_ref, dy1_ref, gout_ref, gup_ref, gdown_ref, small24_ref, small96_ref,
    f_t, du, h2_t, dy, dz, o_t, wout_ref, wup_ref, wdown_ref, flat, load, store,
):
    step = pl.program_id(0)
    steps = pl.num_programs(0)
    rows_at = pl.multiple_of(step * MID, MID)
    here = pl.ds(rows_at, MID)
    chunk = 768
    weights = ((wout_all, wout_ref), (wup_all, wup_ref), (wdown_all, wdown_ref))
    loads = [pltpu.make_async_copy(a, b, load.at[i]) for i, (a, b) in enumerate(weights)]

    @pl.when(step == 0)
    def _():
        for copy in loads:
            copy.start()
        small24_ref[...] = jnp.zeros_like(small24_ref)
        small96_ref[...] = jnp.zeros_like(small96_ref)
        loads[0].wait()

    attended = o_ref[...]
    y1 = x_ref[...].astype(F32) + nn(attended, wout_ref[...]) + vec24_ref[2:3, :]
    normed, inverse = norm_parts(y1)
    h2 = (normed * vec24_ref[3:4, :] + vec24_ref[4:5, :]).astype(BF16)
    rows = lax.broadcasted_iota(jnp.int32, (MID, D), 0) + rows_at
    upstream = jnp.where(rows < len_ref[0], cot_ref[...].astype(F32), 0.0)
    upstream16 = upstream.astype(BF16)
    h2_t[:, here] = h2.T
    o_t[:, here] = attended.T
    dy[here, :] = upstream16
    small24_ref[5:6, :] += jnp.sum(upstream, axis=0, keepdims=True)

    @pl.when(step == 0)
    def _():
        loads[1].wait()
        loads[2].wait()

    y = y1 + vec24_ref[5:6, :]
    dh2 = None
    for c in range(FF // CHUNK):
        cols = slice(c * CHUNK, (c + 1) * CHUNK)
        u = nn(h2, wup_ref[:, cols]) + vec96_ref[7:8, cols]
        square = u * u
        t = jnp.tanh(u * (0.7978845608028654 + 0.035677408136300125 * square))
        half = 0.5 * (1.0 + t)
        f = (u * half).astype(BF16)
        slope = half + (0.5 * u) * (1.0 - t * t) * (
            0.7978845608028654 + 0.10703222440890037 * square
        )
        y = y + nn(f, wdown_ref[cols, :])
        df = nt(upstream16, wdown_ref[cols, :])
        d16 = (df * slope).astype(BF16)
        du[here, cols] = d16
        f_t[cols, here] = f.T
        small96_ref[7:8, cols] += jnp.sum(d16.astype(F32), axis=0, keepdims=True)
        part = nt(d16, wup_ref[:, cols])
        dh2 = part if c == 0 else dh2 + part
    mixed_ref[...] = y.astype(BF16)
    e = dh2 * vec24_ref[3:4, :]
    dy1 = dy[here, :].astype(F32) + norm_back(e, normed, inverse)
    dz16 = dy1.astype(BF16)
    dy1_ref[...] = dy1
    do_ref[...] = nt(dz16, wout_ref[...]).astype(BF16)
    small24_ref[2:3, :] += jnp.sum(dz16.astype(F32), axis=0, keepdims=True)
    small24_ref[3:4, :] += jnp.sum(dh2 * normed, axis=0, keepdims=True)
    small24_ref[4:5, :] += jnp.sum(dh2, axis=0, keepdims=True)
    dz[here, :] = dz16

    @pl.when(step == steps - 1)
    def _():
        shards = gout_ref.shape[0]

        def pipeline(count, stage, compute, target):
            def one(k, carry):
                slot = lax.rem(k, 2)
                copy = pltpu.make_async_copy(stage.at[slot], target(k), store.at[slot])

                @pl.when(k >= 2)
                def _():
                    copy.wait()

                stage[slot] = compute(k)
                copy.start()
                return carry

            lax.fori_loop(0, count, one, 0)
            for k in (count - 2, count - 1):
                pltpu.make_async_copy(stage.at[k % 2], target(k), store.at[k % 2]).wait()

        def blocks(value, depth):
            return value.reshape(value.shape[0] // depth, depth, value.shape[1]).astype(BF16)

        def block(k):
            return pl.ds(pl.multiple_of(k * chunk, chunk), chunk)

        pipeline(
            4,
            flat,
            lambda k: blocks(nn(f_t[block(k), :], dy[...]), D // shards),
            lambda k: gdown_ref.at[pl.ds(k * shards, shards)],
        )
        pipeline(
            4,
            flat,
            lambda k: blocks(nn(h2_t[...], du[:, block(k)]), D // shards),
            lambda k: gup_ref.at[:, :, block(k)],
        )
        flat[0] = blocks(nn(o_t[...], dz[...]), D // shards)
        last = pltpu.make_async_copy(flat.at[0], gout_ref, store.at[0])
        last.start()
        last.wait()


def middle_call(lengths, x, attended, cotangent, vec24, vec96, wout, wup, wdown, shards):
    length = x.shape[0]

    def rows(width):
        return pl.BlockSpec((MID, width), lambda i: (i, 0))

    def whole(shape):
        return pl.BlockSpec(shape, lambda i: (0,) * len(shape), pipeline_mode=pl.Buffered(1))

    anywhere = pl.BlockSpec(memory_space=pl.ANY)
    outs = (
        ((length, D), BF16, rows(D)),
        ((length, D), BF16, rows(D)),
        ((length, D), F32, rows(D)),
        ((shards, D // shards, D), BF16, anywhere),
        ((shards, D // shards, FF), BF16, anywhere),
        ((FF // D * shards, D // shards, D), BF16, anywhere),
        ((16, D), F32, whole((16, D))),
        ((16, FF), F32, whole((16, FF))),
    )
    return pl.pallas_call(
        middle_kernel,
        grid=(length // MID,),
        out_shape=tuple(jax.ShapeDtypeStruct(s, t) for s, t, _ in outs),
        in_specs=[
            pl.BlockSpec(memory_space=pltpu.SMEM),
            rows(D), rows(D), rows(D),
            whole(vec24.shape), whole(vec96.shape),
            anywhere, anywhere, anywhere,
        ],
        out_specs=tuple(b for _, _, b in outs),
        scratch_shapes=[
            VMEM((FF, length), BF16),
            VMEM((length, FF), BF16),
            VMEM((D, length), BF16),
            VMEM((length, D), BF16),
            VMEM((length, D), BF16),
            VMEM((D, length), BF16),
            VMEM(wout.shape, BF16),
            VMEM(wup.shape, BF16),
            VMEM(wdown.shape, BF16),
            VMEM((2, shards, D // shards, D), BF16),
            pltpu.SemaphoreType.DMA((3,)),
            pltpu.SemaphoreType.DMA((2,)),
        ],
        compiler_params=pltpu.CompilerParams(
            dimension_semantics=("arbitrary",), vmem_limit_bytes=63 * 2**20
        ),
    )(lengths, x, attended, cotangent, vec24, vec96, wout, wup, wdown)


def tail_rows(block, x_ref, dy1_ref, vec24_ref, wqkv_ref, dqkv_ref, h1_t, gx_ref, s24_ref, s72_ref):
    here = pl.ds(pl.multiple_of(block * BLK, BLK), BLK)
    normed, inverse = norm_parts(x_ref[here, :].astype(F32))
    if h1_t is not None:
        h1_t[:, here] = (normed * vec24_ref[0:1, :] + vec24_ref[1:2, :]).astype(BF16).T
    grad = dqkv_ref[here, :]
    dh1 = nt(grad, wqkv_ref[...])
    e = dh1 * vec24_ref[0:1, :]
    gx_ref[here, :] = (dy1_ref[here, :] + norm_back(e, normed, inverse)).astype(BF16)
    s24_ref[0:1, :] += jnp.sum(dh1 * normed, axis=0, keepdims=True)
    s24_ref[1:2, :] += jnp.sum(dh1, axis=0, keepdims=True)
    s72_ref[6:7, :] += jnp.sum(grad.astype(F32), axis=0, keepdims=True)


def backward_kernel(
    x_ref, dy1_ref, vec24_ref, wqkv_ref, qkv_ref, o_ref, do_ref, lse_ref,
    gx_ref, gqkv_ref, s24_ref, s72_ref,
    dqkv, h1_t, kt, dk, dv,
):
    s24_ref[...] = jnp.zeros_like(s24_ref)
    s72_ref[...] = jnp.zeros_like(s72_ref)
    lax.fori_loop(
        0,
        HEADS // 2,
        lambda p, c: (
            attention_back_pair(p, qkv_ref, o_ref, do_ref, lse_ref, dqkv, kt, dk, dv),
            c,
        )[1],
        0,
    )
    lax.fori_loop(
        0,
        x_ref.shape[0] // BLK,
        lambda b, c: (
            tail_rows(
                b, x_ref, dy1_ref, vec24_ref, wqkv_ref, dqkv, h1_t, gx_ref, s24_ref, s72_ref
            ),
            c,
        )[1],
        0,
    )
    shards = gqkv_ref.shape[0]
    many = shards // 4

    def one(i, carry):
        left = pl.ds(pl.multiple_of(i * (D // 4), D // 4), D // 4)
        for part in range(3):
            cols = slice(part * D, (part + 1) * D)
            value = nn(h1_t[left, :], dqkv[:, cols]).reshape(many, D // shards, D)
            gqkv_ref[pl.ds(i * many, many), :, cols] = value.astype(BF16)
        return carry

    lax.fori_loop(0, 4, one, 0)


def backward_call(x, dy1, vec24, wqkv, qkv, attended, grad_attended, lse, shards):
    length = x.shape[0]
    return pl.pallas_call(
        backward_kernel,
        out_shape=(
            jax.ShapeDtypeStruct((length, D), BF16),
            jax.ShapeDtypeStruct((shards, D // shards, 3 * D), BF16),
            jax.ShapeDtypeStruct((16, D), F32),
            jax.ShapeDtypeStruct((16, 3 * D), F32),
        ),
        in_specs=[pl.BlockSpec(memory_space=VMEM)] * 8,
        out_specs=(pl.BlockSpec(memory_space=VMEM),) * 4,
        scratch_shapes=[
            VMEM((length, 3 * D), BF16),
            VMEM((D, length), BF16),
            VMEM((128, length), BF16),
            VMEM((length, 128), F32),
            VMEM((length, 128), F32),
        ],
        compiler_params=pltpu.CompilerParams(vmem_limit_bytes=60 * 2**20),
    )(x, dy1, vec24, wqkv, qkv, attended, grad_attended, lse)


def place():
    wide = lax.axis_index("wide")
    return wide // 4, (wide // 2) % 2, wide % 2, lax.axis_index("narrow")


def device(z, x, c, y):
    return ((z * 2 + x) * 2 + c, y)


def greet():
    z, x, c, y = place()
    barrier = pltpu.get_barrier_semaphore()
    peers = [device(lax.rem(z + d, 4), x, c, y) for d in (1, 2, 3)]
    peers += [device(z, 1 - x, c, y), device(z, x, c, 1 - y), device(z, x, 1 - c, y)]
    for peer in peers:
        pl.semaphore_signal(barrier, inc=1, device_id=peer, device_id_type=MESH)
    pl.semaphore_wait(barrier, len(peers))


def remote(src, dst, sems, slot, peer):
    return pltpu.make_async_remote_copy(
        src_ref=src, dst_ref=dst, send_sem=sems[0].at[slot], recv_sem=sems[1].at[slot],
        device_id=peer, device_id_type=MESH,
    )


FIRST_Z = (("z", "x", "y"), ("z", "y", "x"))
LATER_Z = (("x", "z", "y"), ("y", "z", "x"))
UP_ORDERS = FIRST_Z
DOWN_ORDERS = LATER_Z


def peers_of(z, x, c, y):
    return {
        "z": [device(lax.rem(z + d, 4), x, c, y) for d in (1, 2, 3)],
        "x": [device(z, 1 - x, c, y)],
        "y": [device(z, x, c, 1 - y)],
        "c": [device(z, x, 1 - c, y)],
    }


def halves(low, high):
    cut = (high - low) // 256 * 128
    return [(low, low + cut), (low + cut, high)] if cut else [(low, high)]


def window(span):
    return pl.ds(span[0], span[1] - span[0])


class Gather:
    slots = 16

    def __init__(self, own, full, sems, local, rows=None, cols=None, orders=FIRST_Z):
        height, width = full.shape[-2:]
        span = cols or (0, width)
        rows = slice(None) if rows is None else window(rows)
        z, x, c, y = place()
        here = {"z": z, "x": x, "y": y}
        peers = peers_of(z, x, c, y)
        lanes = list(zip(halves(*span), orders))
        self.groups = [[], [], []]
        self.core = [[], [], [], []]
        slot = 0

        def at(state, cols):
            return full.at[state["z"], state["x"], c, state["y"], rows, window(cols)]

        for k in range(3):
            items = lanes
            if k == 0 and all(order[0] == orders[0][0] for _, order in lanes):
                items = [(span, orders[0])]
            for cols, order in items:
                now = {d: slice(None) if d in order[:k] else here[d] for d in "zxy"}
                source = own.at[rows, window(cols)] if k == 0 else at(now, cols)
                for peer in peers[order[k]]:
                    self.groups[k].append(remote(source, at(now, cols), sems, slot, peer))
                    slot += 1
                if "z" in order[: k + 1]:
                    later = dict(now)
                    later[order[k]] = slice(None) if order[k] == "z" else 1 - here[order[k]]
                    view = at(later, cols)
                    self.core[k + 1].append(remote(view, view, sems, slot, peers["c"][0]))
                    slot += 1
        self.kept = pltpu.make_async_copy(own.at[rows, window(span)], at(here, span), local)

    def run(self, stage):
        if stage == 0:
            self.kept.start()
        elif stage == 1:
            self.kept.wait()
        if 1 <= stage <= 3:
            for copy in self.groups[stage - 1]:
                copy.wait_recv()
        if stage <= 2:
            for copy in self.groups[stage]:
                copy.start()
        if stage <= 3:
            for copy in self.core[stage]:
                copy.start()
        every_core = [copy for copies in self.core for copy in copies]
        if stage == 4:
            for copy in every_core:
                copy.wait_recv()
        if stage == 5:
            for copy in every_core + [copy for copies in self.groups for copy in copies]:
                copy.wait_send()


def spread(blocks, each):
    width = 32 * each
    lane = lax.broadcasted_iota(jnp.int32, (128, width), 0)
    col = lax.broadcasted_iota(jnp.int32, (128, width), 1)
    value = nn(blocks, (lax.rem(col, each) == lane).astype(BF16)).reshape(32, 16, width)
    shard = lax.broadcasted_iota(jnp.int32, (32, 16, width), 0)
    col = lax.broadcasted_iota(jnp.int32, (32, 16, width), 2)
    inside = (col >= shard * each) & (col < shard * each + each)
    return jnp.sum(jnp.where(inside, value, 0.0), axis=0)


FORWARD = {
    "n": ("X0", "S0", "Y0",),
    "h": ("Z0", "X1", "S1", "O0", "X2", "U0", "S2", "Y1", "D0", "X3", "S3", "S4", "Y2",),
    0: ("X4", "Z1", "V0", "O1", "E0",),
    1: ("Y3", "Z2",),
    3: ("O2",),
    5: ("Z3", "U1", "D1",),
    8: ("O3",),
    9: ("V1",),
    10: ("Y4", "U2",),
    14: ("V2", "E1",),
    15: ("U3",),
    20: ("Z4", "D2",),
    21: ("V3",),
    24: ("E2",),
    25: ("D3",),
    "last": ("E3", "O4", "U4", "D4", "V4", "E4",),
}


def runner(parts, table):
    def run(at):
        for word in table.get(at, ()):
            parts[word[0]].run(int(word[1]))

    return run


def when_run(run, table, value, positions):
    for number, at in positions:
        if at in table:

            @pl.when(value == number)
            def _():
                run(at)


def gather_forward_kernel(
    x_ref, small_ref, wqkv_own, wout_own, wup_own, wdown_own,
    wqkv_out, wout_full, wup_full, wdown_full, vec24_ref, vec96_ref, qkv_out, o_out, lse_ref,
    small_full, wqkv_full, vec72, own_groups, hidden, vt, wqkv_ref, qkv_ref, o_ref,
    send, recv, local, store,
):
    greet()
    results = ((wqkv_ref, wqkv_out), (qkv_ref, qkv_out), (o_ref, o_out))
    stores = [pltpu.make_async_copy(a, b, store.at[i]) for i, (a, b) in enumerate(results)]
    length = x_ref.shape[0]
    steps = length // BLK
    half = wdown_full.shape[-2] // 2
    parts = {}

    def add_part(name, own, full, **view):
        i = len(parts)
        parts[name] = Gather(own, full, (send.at[i], recv.at[i]), local.at[i], **view)

    add_part("S", small_ref, small_full)
    for group, name in enumerate("XYZ"):
        add_part(name, own_groups, wqkv_full, cols=(group * D, (group + 1) * D))
        for part in range(3):
            own_groups[:, (3 * group + part) * 256 : (3 * group + part + 1) * 256] = wqkv_own[
                :, part * D + group * 256 : part * D + (group + 1) * 256
            ]
    add_part("O", wout_own, wout_full)
    add_part("U", wup_own, wup_full, cols=(0, FF // 2), orders=UP_ORDERS)
    add_part("V", wup_own, wup_full, cols=(FF // 2, FF), orders=UP_ORDERS)
    add_part("D", wdown_own, wdown_full, rows=(0, half), orders=DOWN_ORDERS)
    add_part("E", wdown_own, wdown_full, rows=(half, 2 * half), orders=DOWN_ORDERS)
    run = runner(parts, FORWARD)
    run("n")

    def normalize(block, carry):
        here = pl.ds(pl.multiple_of(block * BLK, BLK), BLK)
        normed, _ = norm_parts(x_ref[here, :].astype(F32))
        hidden[here, :] = (normed * vec24_ref[0:1, :] + vec24_ref[1:2, :]).astype(BF16)
        return carry

    run("h")
    blocks = small_full[...].reshape(32 * 16, 128)
    for ref, each in zip((vec24_ref, vec72, vec96_ref), (24, 72, 96)):
        ref[...] = spread(blocks, each)
    lax.fori_loop(0, steps, normalize, 0)

    def group_qkv(group):
        wide = pl.ds(pl.multiple_of(group * D, D), D)

        def spot(part):
            return pl.ds(pl.multiple_of(part * D + group * 256, 256), 256)

        def flatten(i, carry):
            two = wqkv_full[i // 4, (i // 2) % 2, i % 2, :, :, wide].astype(F32)
            two = two.reshape(D // 16, D).astype(BF16)
            rows = pl.ds(pl.multiple_of(i * (D // 16), D // 16), D // 16)
            for part in range(3):
                wqkv_ref[rows, spot(part)] = two[:, part * 256 : (part + 1) * 256]
            return carry

        lax.fori_loop(0, 16, flatten, 0)

        def rows_qkv(block, carry):
            here = pl.ds(pl.multiple_of(block * BLK, BLK), BLK)
            for part in range(3):
                value = nn(hidden[here, :], wqkv_ref[:, spot(part)]) + vec72[6:7, spot(part)]
                qkv_ref[here, spot(part)] = value.astype(BF16)
            return carry

        lax.fori_loop(0, steps, rows_qkv, 0)

    def one(pair, carry):
        def event(j):
            spots = [(p, p * (steps + 1) + 1 + j) for p in range(HEADS // 2)]
            when_run(run, FORWARD, pair, spots)

        event(-1)

        @pl.when(pair % 2 == 0)
        def _():
            group_qkv(pair // 2)

        attention_pair(pair, qkv_ref, o_ref, lse_ref, vt, event)
        return carry

    lax.fori_loop(0, HEADS // 2, one, 0)
    for copy in stores:
        copy.start()
    run("last")
    for part in parts.values():
        part.run(5)
    for copy in stores:
        copy.wait()


def gather_forward_call(x, small, wqkv, wout, wup, wdown):
    length = x.shape[0]
    anywhere = pl.BlockSpec(memory_space=pl.ANY)
    inside = pl.BlockSpec(memory_space=VMEM)

    def full(own):
        return jax.ShapeDtypeStruct((4, 2, 2, 2, *own.shape), BF16)

    return pl.pallas_call(
        gather_forward_kernel,
        out_shape=(
            jax.ShapeDtypeStruct((D, 3 * D), BF16),
            full(wout), full(wup), full(wdown),
            jax.ShapeDtypeStruct((16, D), F32),
            jax.ShapeDtypeStruct((16, FF), F32),
            jax.ShapeDtypeStruct((length, 3 * D), BF16),
            jax.ShapeDtypeStruct((length, D), BF16),
            jax.ShapeDtypeStruct((HEADS // 2, 8, length), F32),
        ),
        in_specs=[inside] * 3 + [anywhere] * 3,
        out_specs=(*[anywhere] * 4, inside, inside, anywhere, anywhere, inside),
        scratch_shapes=[
            VMEM((4, 2, 2, 2, 16, 128), BF16),
            VMEM((4, 2, 2, 2, *wqkv.shape), BF16),
            VMEM((16, 3 * D), F32),
            VMEM(wqkv.shape, BF16),
            VMEM((length, D), BF16),
            VMEM((128, length), BF16),
            VMEM((D, 3 * D), BF16),
            VMEM((length, 3 * D), BF16),
            VMEM((length, D), BF16),
            pltpu.SemaphoreType.DMA((9, Gather.slots)),
            pltpu.SemaphoreType.DMA((9, Gather.slots)),
            pltpu.SemaphoreType.DMA((9,)),
            pltpu.SemaphoreType.DMA((3,)),
        ],
        compiler_params=pltpu.CompilerParams(
            collective_id=1, has_side_effects=True, vmem_limit_bytes=60 * 2**20
        ),
    )(x, small, wqkv, wout, wup, wdown)


SIZES = {"z": 4, "x": 2, "y": 2}


def held_after(order, k):
    return [d for d in "zxy" if d not in order[:k]]


class Scatter:
    slots = 12

    def __init__(self, grads, buffers, sems, local, put, rows=None, cols=None, orders=FIRST_Z):
        height, width = grads.shape[-2:]
        low, high = cols or (0, width)
        rows = slice(None) if rows is None else window(rows)
        cols = slice(None) if cols is None else window(cols)
        z, x, c, y = place()
        self.here = {"z": z, "x": x, "y": y}
        self.core_at = c
        peers = peers_of(z, x, c, y)
        self.grads, self.put = grads, put
        self.mine, self.one, *rest = buffers
        if self.mine is not None:
            self.kept = pltpu.make_async_copy(grads.at[:, :, c, :, rows, cols], self.mine, local)
        self.groups = [[remote(grads.at[:, :, 1 - c, :, rows, cols], self.one, sems, 0, peers["c"][0])]]
        self.groups += [[], [], []]
        self.lanes = []
        slot = 1
        for span, order in zip(halves(0, high - low), orders):
            order = order[::-1]
            got = [rest.pop(0) for _ in range(3)]
            self.lanes.append((window(span), order, got))
            for k in range(3):
                source = self.one if k == 0 else got[k - 1]
                cut = (slice(None), window(span)) if k == 0 else (slice(None), slice(None))
                if k > 0 and order[k - 1] == "z":
                    source = source.at[0]
                if order[k] == "z":
                    others = [lax.rem(z + d, 4) for d in (1, 2, 3)]
                else:
                    others = [1 - self.here[order[k]]]
                for i, (other, peer) in enumerate(zip(others, peers[order[k]])):
                    index = [other if d == order[k] else slice(None) for d in held_after(order, k)]
                    target = got[k].at[i] if order[k] == "z" else got[k]
                    self.groups[k + 1].append(
                        remote(source.at[(*index, *cut)], target, sems, slot, peer)
                    )
                    slot += 1

    @staticmethod
    def shapes(r, n, mine, orders=FIRST_Z):
        result = [VMEM((4, 2, 2, r, n), BF16)] * (2 if mine else 1)
        for (low, high), order in zip(halves(0, n), orders):
            order = order[::-1]
            for k in range(3):
                held = [SIZES[d] for d in held_after(order, k + 1)]
                lead = [3] if order[k] == "z" else []
                result.append(VMEM((*lead, *held, r, high - low), BF16))
        return result

    def add(self, lane, k):
        cols, order, got = lane
        before = held_after(order, k)
        after = held_after(order, k + 1)

        def total(index):
            at = dict(zip(after, index))
            at[order[k]] = self.here[order[k]]
            where = tuple(at[d] for d in before)
            if k == 0:
                value = self.one[(*where, slice(None), cols)]
            else:
                lead = (0,) if order[k - 1] == "z" else ()
                value = got[k - 1][(*lead, *where)]
            lead = [(i,) for i in range(3)] if order[k] == "z" else [()]
            if k == 2:
                value = value.astype(F32)
                for i in lead:
                    value = value + got[k][i + index].astype(F32)
                return value
            for i in lead:
                value = value + got[k][i + index]
            got[k][lead[0] + index] = value

        if not after:
            return total(())
        sizes = [SIZES[d] for d in after]

        def loop(i, carry):
            if len(sizes) == 1:
                total((i,))
            else:
                for j in range(sizes[1]):
                    total((i, j))
            return carry

        lax.fori_loop(0, sizes[0], loop, 0)

    def run(self, stage):
        if stage == 0 and self.mine is not None:
            self.kept.start()
        if stage == 1 and self.mine is not None:
            self.kept.wait()
        if 1 <= stage <= 4:
            for copy in self.groups[stage - 1]:
                copy.wait_recv()
        if stage == 1:

            def add(i, carry):
                a, b = i // 2, i % 2
                own = self.grads[a, b, self.core_at] if self.mine is None else self.mine[a, b]
                self.one[a, b] = self.one[a, b] + own
                return carry

            lax.fori_loop(0, 8, add, 0)
        if stage in (2, 3):
            for lane in self.lanes:
                self.add(lane, stage - 2)
        if stage == 4:
            values = [self.add(lane, 2) for lane in self.lanes]
            self.put(values[0] if len(values) == 1 else jnp.concatenate(values, axis=1))
        if stage <= 3:
            for copy in self.groups[stage]:
                copy.start()
        if stage == 5:
            for copies in self.groups:
                for copy in copies:
                    copy.wait_send()


def fold(values, each, row):
    width = 32 * each
    shard = lax.broadcasted_iota(jnp.int32, (32, 16, width), 0)
    col = lax.broadcasted_iota(jnp.int32, (32, 16, width), 2)
    inside = (col >= shard * each) & (col < shard * each + each)
    spreaded = jnp.where(inside, values[None], 0.0).reshape(32 * 16, width).astype(BF16)
    lane = lax.broadcasted_iota(jnp.int32, (128, width), 0)
    col = lax.broadcasted_iota(jnp.int32, (128, width), 1)
    return nt(spreaded, (lax.rem(col, each) == lane).astype(BF16))


BACKWARD = {
    "h": ("D0", "E0", "U0",),
    0: ("V0", "O0",),
    1: ("D1",),
    5: ("E1",),
    6: ("D2",),
    "g0": ("X0", "U1",),
    10: ("V1",),
    12: ("E2",),
    14: ("D3", "U2",),
    "g1": ("V2", "Y0",),
    17: ("O1", "U3",),
    18: ("X1",),
    20: ("E3",),
    21: ("V3", "O2", "X2",),
    22: ("Y1",),
    23: ("O3",),
    "t0": ("Z0",),
    "t1": ("X3", "Y2", "Z1",),
    "t3": ("Y3",),
    "f": ("Z2",),
    "e": ("S0",),
    "last": ("S1", "Z3", "S2", "S3", "D4", "E4", "U4", "V4", "O4", "X4", "Y4", "Z4", "S4",),
}
GROUPS = 3


def scatter_backward_kernel(
    x_all, dy1_all, vec24_ref, wqkv_all, qkv_all, o_all, do_all, lse_ref, s24_mid, s96_mid,
    gout_all, gup_all, gdown_all,
    gx_ref, gqkv_ref, gout_ref, gup_ref, gdown_ref, small_ref,
    dqkv, h1_t, kt, dk, dv, s24_ref, s72_ref, small_all,
    x_ref, qkv_ref, do_ref, o_ref, dy1_ref, wqkv_ref, *buffers,
):
    send, recv, local, load = buffers[-4:]
    buffers = list(buffers[:-4])
    greet()
    inputs = (
        (x_all, x_ref), (qkv_all, qkv_ref), (do_all, do_ref), (o_all, o_ref), (dy1_all, dy1_ref),
        (wqkv_all, wqkv_ref),
    )
    loads = [pltpu.make_async_copy(a, b, load.at[i]) for i, (a, b) in enumerate(inputs)]
    half = gdown_all.shape[-2] // 2
    parts = {}

    def add_part(name, grads, mine, put, **view):
        i = len(parts)
        held = [buffers.pop(0)] if mine else [None]
        count = 4 if len(halves(0, grads.shape[-1])) == 1 else 7
        held += [buffers.pop(0) for _ in range(count)]
        parts[name] = Scatter(grads, held, (send.at[i], recv.at[i]), local.at[i], put, **view)

    def put_at(ref, rows, cols):
        def put(value):
            ref[rows, cols] = value

        return put

    every = slice(None)
    for name, k in (("U", 0), ("V", 1)):
        cols = (k * FF // 2, (k + 1) * FF // 2)
        add_part(name, gup_all, True, put_at(gup_ref, every, slice(*cols)), cols=cols, orders=UP_ORDERS)
    for name, k in (("D", 0), ("E", 1)):
        rows = (k * half, (k + 1) * half)
        add_part(name, gdown_all, True, put_at(gdown_ref, slice(*rows), every), rows=rows, orders=DOWN_ORDERS)
    add_part("O", gout_all, True, put_at(gout_ref, every, every))
    groups = [buffers.pop(0) for _ in range(GROUPS)]

    def put_group(group):
        def put(value):
            for part in range(3):
                low = part * D + group * 256
                gqkv_ref[:, low : low + 256] = value[:, part * 256 : (part + 1) * 256]

        return put

    for group, name in enumerate("XYZ"):
        add_part(name, groups[group], False, put_group(group))
    add_part("S", small_all, False, put_at(small_ref, every, every))

    run = runner(parts, BACKWARD)
    run("h")
    for copy in loads:
        copy.start()
    s24_ref[...] = jnp.zeros_like(s24_ref)
    s72_ref[...] = jnp.zeros_like(s72_ref)
    length = x_ref.shape[0]
    steps = length // BLK

    def hidden_rows(block, carry):
        here = pl.ds(pl.multiple_of(block * BLK, BLK), BLK)
        normed, _ = norm_parts(x_ref[here, :].astype(F32))
        hidden = (normed * vec24_ref[0:1, :] + vec24_ref[1:2, :]).astype(BF16)
        h1_t[:, here] = hidden.T
        return carry

    loads[0].wait()
    lax.fori_loop(0, steps, hidden_rows, 0)
    for copy in loads[1:4]:
        copy.wait()

    def group_grads(group):
        def one(i, carry):
            left = pl.ds(pl.multiple_of(i * (D // 4), D // 4), D // 4)
            for part in range(3):
                low = part * D + group * 256
                value = nn(h1_t[left, :], dqkv[:, low : low + 256])
                value = value.reshape(2, 2, 2, D // 32, 256).astype(BF16)
                groups[group][i, :, :, :, :, part * 256 : (part + 1) * 256] = value
            return carry

        lax.fori_loop(0, 4, one, 0)

    def one(pair, carry):
        def event(j):
            at_step = steps - 1 - j
            if at_step == 0:
                for group in range(GROUPS - 1):

                    @pl.when(pair == 2 * group + 2)
                    def _():
                        group_grads(group)
                        run(f"g{group}")

            spots = [(p, p * steps + at_step) for p in range(HEADS // 2)]
            when_run(run, BACKWARD, pair, spots)

        attention_back_pair(pair, qkv_ref, o_ref, do_ref, lse_ref, dqkv, kt, dk, dv, event)
        return carry

    lax.fori_loop(0, HEADS // 2, one, 0)
    run("g2")
    group_grads(GROUPS - 1)
    for copy in loads[4:]:
        copy.wait()

    def tail(block, carry):
        when_run(run, BACKWARD, block, [(b, f"t{b}") for b in range(steps)])
        tail_rows(block, x_ref, dy1_ref, vec24_ref, wqkv_ref, dqkv, None, gx_ref, s24_ref, s72_ref)
        return carry

    lax.fori_loop(0, steps, tail, 0)
    run("f")
    total = fold(s24_ref[...] + s24_mid[...], 24, 0)
    total = total + fold(s72_ref[...], 72, 6) + fold(s96_mid[...], 96, 7)
    small_all[...] = total.reshape(4, 2, 2, 2, 16, 128).astype(BF16)
    run("e")
    run("last")
    for part in parts.values():
        part.run(5)


def scatter_backward_call(
    x, dy1, vec24, wqkv, qkv, attended, grad_attended, lse, s24, s96, gout, gup, gdown
):
    length = x.shape[0]
    anywhere = pl.BlockSpec(memory_space=pl.ANY)
    inside = pl.BlockSpec(memory_space=VMEM)
    deep = gdown.shape[-2]
    scratch = [
        VMEM((length, 3 * D), BF16),
        VMEM((D, length), BF16),
        VMEM((128, length), BF16),
        VMEM((length, 128), F32),
        VMEM((length, 128), F32),
        VMEM((16, D), F32),
        VMEM((16, 3 * D), F32),
        VMEM((4, 2, 2, 2, 16, 128), BF16),
        VMEM((length, D), BF16),
        VMEM((length, 3 * D), BF16),
        VMEM((length, D), BF16),
        VMEM((length, D), BF16),
        VMEM((length, D), F32),
        VMEM((D, 3 * D), BF16),
    ]
    for _ in range(2):
        scratch += Scatter.shapes(D // 32, FF // 2, True, UP_ORDERS)
    for _ in range(2):
        scratch += Scatter.shapes(deep // 2, D, True, DOWN_ORDERS)
    scratch += Scatter.shapes(D // 32, D, True)
    scratch += [VMEM((4, 2, 2, 2, D // 32, D), BF16)] * GROUPS
    for _ in range(GROUPS):
        scratch += Scatter.shapes(D // 32, D, False)
    scratch += Scatter.shapes(16, 128, False)
    scratch += [pltpu.SemaphoreType.DMA((9, Scatter.slots))] * 2 + [pltpu.SemaphoreType.DMA((9,))]
    scratch += [pltpu.SemaphoreType.DMA((6,))]
    return pl.pallas_call(
        scatter_backward_kernel,
        out_shape=(
            jax.ShapeDtypeStruct((length, D), BF16),
            jax.ShapeDtypeStruct((D // 32, 3 * D), F32),
            jax.ShapeDtypeStruct((D // 32, D), F32),
            jax.ShapeDtypeStruct((D // 32, FF), F32),
            jax.ShapeDtypeStruct((deep, D), F32),
            jax.ShapeDtypeStruct((16, 128), F32),
        ),
        in_specs=[
            anywhere, anywhere, inside, *[anywhere] * 4, inside, inside, inside, *[anywhere] * 3
        ],
        out_specs=(inside,) * 6,
        scratch_shapes=scratch,
        compiler_params=pltpu.CompilerParams(
            collective_id=2, has_side_effects=True, vmem_limit_bytes=63 * 2**20
        ),
    )(x, dy1, vec24, wqkv, qkv, attended, grad_attended, lse, s24, s96, gout, gup, gdown)


def finish_kernel(
    gx, gqkv, gout, gup, gdown, small, gx_out, gqkv_out, gout_out, gup_out, gdown_out, *vectors
):
    gx_out[...] = gx[...]
    gqkv_out[...] = gqkv[...]
    gout_out[...] = gout[...]
    gup_out[...] = gup[...]
    gdown_out[...] = gdown[...]
    for row, out in enumerate(vectors):
        out[...] = small[row, 0 : out.shape[0]]


def finish_call(mixed, gx, gqkv, gout, gup, gdown, small, shapes):
    inside = pl.BlockSpec(memory_space=VMEM)
    whole = (gqkv, gout, gup, gdown)
    outs = [jax.ShapeDtypeStruct(gx.shape, gx.dtype)]
    outs += [jax.ShapeDtypeStruct(a.shape, F32) for a in whole]
    outs += [jax.ShapeDtypeStruct(shape, F32) for shape in shapes]
    gx, gqkv, gout, gup, gdown, *folded = pl.pallas_call(
        finish_kernel,
        out_shape=tuple(outs),
        in_specs=[inside] * 6,
        out_specs=(inside,) * len(outs),
        compiler_params=pltpu.CompilerParams(vmem_limit_bytes=60 * 2**20),
    )(gx, *whole, small)
    return (
        mixed, gx, folded[0], folded[1], gqkv, folded[6], gout, folded[2], folded[3], folded[4],
        gup, folded[7], gdown, folded[5],
    )


def shards(
    tokens, cotangent, lengths, ln1_gain, ln1_shift, qkv_weight, qkv_bias, out_weight, out_bias,
    ln2_gain, ln2_shift, up_weight, up_bias, down_weight, down_bias, *, special,
):
    vectors = (ln1_gain, ln1_shift, out_bias, ln2_gain, ln2_shift, down_bias, qkv_bias, up_bias)
    if special:
        small = jnp.stack(
            [jnp.pad(v, (0, 128 - v.shape[0])) for v in vectors] + [jnp.zeros((128,), BF16)] * 8
        )
        wqkv, wout, wup, wdown, vec24, vec96, qkv, attended, lse = gather_forward_call(
            tokens, small, qkv_weight, out_weight, up_weight, down_weight
        )
        wout, wup = (w.reshape(D, w.shape[-1]) for w in (wout, wup))
        wdown = wdown.reshape(FF, D)
    else:
        gather = functools.partial(lax.all_gather, axis_name=AXES, axis=0, tiled=True)
        wqkv, wout, wup, wdown = map(gather, (qkv_weight, out_weight, up_weight, down_weight))
        whole = [gather(v).astype(F32) for v in vectors]
        vec24 = jnp.pad(jnp.stack(whole[:6]), ((0, 10), (0, 0)))
        vec72 = jnp.pad(whole[6][None], ((6, 9), (0, 0)))
        vec96 = jnp.pad(whole[7][None], ((7, 8), (0, 0)))
        qkv, attended, lse = forward_call(tokens, vec24, vec72, wqkv)
    mixed, do, dy1, gout, gup, gdown, s24_mid, s96 = middle_call(
        lengths, tokens, attended, cotangent, vec24, vec96, wout, wup, wdown, 32
    )
    if special:
        gout, gup = (g.reshape(4, 2, 2, 2, *g.shape[1:]) for g in (gout, gup))
        gdown = gdown.reshape(4, 2, 2, 2, FF // 32, D)
        gx, gqkv, gout, gup, gdown, small = scatter_backward_call(
            tokens, dy1, vec24, wqkv, qkv, attended, do, lse, s24_mid, s96, gout, gup, gdown
        )
        return finish_call(mixed, gx, gqkv, gout, gup, gdown, small, [v.shape for v in vectors])
    else:
        gx, gqkv, s24, s72 = backward_call(tokens, dy1, vec24, wqkv, qkv, attended, do, lse, 32)
        scatter = functools.partial(
            lax.psum_scatter, axis_name=AXES, scatter_dimension=0, tiled=True
        )
        gqkv, gout, gup = (scatter(g.reshape(D, -1).astype(F32)) for g in (gqkv, gout, gup))
        gdown = scatter(gdown.reshape(FF, D).astype(F32))
        both = s24 + s24_mid
        folded = [scatter(both[i]) for i in range(6)] + [scatter(s72[6]), scatter(s96[7])]
    return (
        mixed, gx, folded[0], folded[1], gqkv, folded[6], gout, folded[2], folded[3], folded[4],
        gup, folded[7], gdown, folded[5],
    )


def solution(mesh):
    flat, rows = P(AXES), P(AXES, None)
    in_specs = (
        rows, rows, flat, flat, flat, rows, flat, rows, flat, flat, flat, rows, flat, rows, flat,
    )
    out_specs = (
        rows, rows, flat, flat, rows, flat, rows, flat, flat, flat, rows, flat, rows, flat,
    )
    special = dict(mesh.shape) == {"wide": 16, "narrow": 2}
    return jax.shard_map(
        functools.partial(shards, special=special),
        mesh=mesh, in_specs=in_specs, out_specs=out_specs, check_vma=False,
    )
```

```python
import functools

import jax
import jax.numpy as jnp
from jax import lax
from jax.experimental import pallas as pl
from jax.experimental.pallas import tpu as pltpu
from jax.sharding import PartitionSpec as P

D = 768
FF = 3072
HEADS = 12
HEAD = 64
BLK = 256
MID = 256
CHUNK = 768
AXES = ("wide", "narrow")
MESH = pl.DeviceIdType.MESH
VMEM = pltpu.VMEM
F32 = jnp.float32
BF16 = jnp.bfloat16


def nn(left, right):
    return lax.dot_general(left, right, (((1,), (0,)), ((), ())), preferred_element_type=F32)


def nt(left, right):
    return lax.dot_general(left, right, (((1,), (1,)), ((), ())), preferred_element_type=F32)


def norm_parts(values):
    average = jnp.mean(values, axis=-1, keepdims=True)
    centered = values - average
    inverse = lax.rsqrt(jnp.mean(centered * centered, axis=-1, keepdims=True) + 1e-05)
    return centered * inverse, inverse


def norm_back(grad_normed, normed, inverse):
    first_mean = jnp.mean(grad_normed, axis=-1, keepdims=True)
    second_mean = jnp.mean(grad_normed * normed, axis=-1, keepdims=True)
    return inverse * (grad_normed - first_mean - normed * second_mean)


def lane_half(values, half):
    lanes = lax.broadcasted_iota(jnp.int32, values.shape, 1)
    keep = (lanes < HEAD) if half == 0 else (lanes >= HEAD)
    return jnp.where(keep, values, jnp.zeros_like(values))


def diagonal_keep():
    keys = lax.broadcasted_iota(jnp.int32, (BLK, BLK), 0)
    queries = lax.broadcasted_iota(jnp.int32, (BLK, BLK), 1)
    return keys <= queries


def column(pair, part):
    return pl.ds(pl.multiple_of(part * D + pair * 128, 128), 128)


def qkv_rows(block, x_ref, vec24_ref, vec72_ref, wqkv_ref, qkv_ref):
    rows = pl.ds(pl.multiple_of(block * BLK, BLK), BLK)
    normed, _ = norm_parts(x_ref[rows, :].astype(F32))
    hidden = (normed * vec24_ref[0:1, :] + vec24_ref[1:2, :]).astype(BF16)
    for part in range(3):
        cols = slice(part * D, (part + 1) * D)
        qkv_ref[rows, cols] = (nn(hidden, wqkv_ref[:, cols]) + vec72_ref[6:7, cols]).astype(BF16)


def attention_pair(pair, qkv_ref, o_ref, lse_ref, vt, event=lambda j: None):
    length = qkv_ref.shape[0]
    vt[...] = qkv_ref[:, column(pair, 2)].T
    keep = diagonal_keep()
    for j in range(length // BLK):
        event(j)
        span = (j + 1) * BLK
        rows = slice(j * BLK, span)
        query = qkv_ref[rows, column(pair, 0)] * jnp.asarray(0.125, BF16)
        keys = qkv_ref[0:span, column(pair, 1)]
        outs = []
        for half in range(2):
            s = nt(keys, lane_half(query, half))
            w = s * s + 1.0
            m = w * lax.rsqrt(w)
            tail = jnp.where(keep, m[j * BLK :], -1e30)
            m = tail if j == 0 else jnp.concatenate([m[: j * BLK], tail], axis=0)
            top = jnp.max(m, axis=0, keepdims=True)
            e = jnp.exp(m - top)
            total = jnp.sum(e, axis=0, keepdims=True)
            a = (jnp.tanh(s) * e).astype(BF16)
            outs.append(nn(vt[half * HEAD : (half + 1) * HEAD, 0:span], a) / total)
            lse_ref[pair, half : half + 1, rows] = top + jnp.log(total)
        o_ref[rows, column(pair, 0)] = jnp.concatenate(outs, axis=0).T.astype(BF16)


def attention_back_pair(
    pair, qkv_ref, o_ref, do_ref, lse_ref, dqkv_ref, kt, dk, dv, event=lambda j: None
):
    length = qkv_ref.shape[0]
    kt[...] = qkv_ref[:, column(pair, 1)].T
    keep = diagonal_keep()
    lanes = lax.broadcasted_iota(jnp.int32, (8, 128), 1)
    sublanes = lax.broadcasted_iota(jnp.int32, (8, 128), 0)
    pick = (lanes // HEAD == sublanes).astype(F32)
    steps = length // BLK
    for j in reversed(range(steps)):
        event(j)
        span = (j + 1) * BLK
        rows = slice(j * BLK, span)
        query = qkv_ref[rows, column(pair, 0)] * jnp.asarray(0.125, BF16)
        grad = do_ref[rows, column(pair, 0)]
        product = grad.astype(F32) * o_ref[rows, column(pair, 0)].astype(F32)
        inner = lax.dot_general(
            pick, product, (((1,), (1,)), ((), ())),
            precision=lax.Precision.HIGHEST, preferred_element_type=F32,
        )
        keys = qkv_ref[0:span, column(pair, 1)]
        values = qkv_ref[0:span, column(pair, 2)]
        dqs = []
        dks = None
        dvs = None
        for half in range(2):
            query_half = lane_half(query, half)
            grad_half = lane_half(grad, half)
            s = nt(keys, query_half)
            da = nt(values, grad_half)
            w = s * s + 1.0
            r = lax.rsqrt(w)
            p = jnp.exp(w * r - lse_ref[pair, half : half + 1, rows])
            tail = jnp.where(keep, p[j * BLK :], 0.0)
            p = tail if j == 0 else jnp.concatenate([p[: j * BLK], tail], axis=0)
            t = jnp.tanh(s)
            a = (t * p).astype(BF16)
            ds = p * (da * (1.0 - t * t) + (da * t - inner[half : half + 1, :]) * (s * r))
            ds = ds.astype(BF16)
            dqs.append(nn(kt[half * HEAD : (half + 1) * HEAD, 0:span], ds))
            this_dk = nn(ds, query_half)
            this_dv = nn(a, grad_half)
            dks = this_dk if half == 0 else dks + this_dk
            dvs = this_dv if half == 0 else dvs + this_dv
        dqkv_ref[rows, column(pair, 0)] = (jnp.concatenate(dqs, axis=0).T * 0.125).astype(BF16)
        if j == steps - 1:
            dk[...] = dks
            dv[...] = dvs
        else:
            dk[0:span, :] += dks
            dv[0:span, :] += dvs
    dqkv_ref[:, column(pair, 1)] = dk[...].astype(BF16)
    dqkv_ref[:, column(pair, 2)] = dv[...].astype(BF16)


def forward_kernel(x_ref, vec24_ref, vec72_ref, wqkv_ref, qkv_ref, o_ref, lse_ref, vt):
    lax.fori_loop(
        0,
        x_ref.shape[0] // BLK,
        lambda b, c: (qkv_rows(b, x_ref, vec24_ref, vec72_ref, wqkv_ref, qkv_ref), c)[1],
        0,
    )
    lax.fori_loop(
        0, HEADS // 2, lambda p, c: (attention_pair(p, qkv_ref, o_ref, lse_ref, vt), c)[1], 0
    )


def forward_call(x, vec24, vec72, wqkv):
    length = x.shape[0]
    return pl.pallas_call(
        forward_kernel,
        out_shape=(
            jax.ShapeDtypeStruct((length, 3 * D), BF16),
            jax.ShapeDtypeStruct((length, D), BF16),
            jax.ShapeDtypeStruct((HEADS // 2, 8, length), F32),
        ),
        in_specs=[pl.BlockSpec(memory_space=VMEM)] * 4,
        out_specs=(pl.BlockSpec(memory_space=VMEM),) * 3,
        scratch_shapes=[VMEM((128, length), BF16)],
        compiler_params=pltpu.CompilerParams(vmem_limit_bytes=56 * 2**20),
    )(x, vec24, vec72, wqkv)


def middle_kernel(
    len_ref, x_ref, o_ref, cot_ref, vec24_ref, vec96_ref, wout_all, wup_all, wdown_all,
    mixed_ref, do_ref, dy1_ref, gout_ref, gup_ref, gdown_ref, small24_ref, small96_ref,
    f_t, du, h2_t, dy, dz, o_t, wout_ref, wup_ref, wdown_ref, flat, load, store,
):
    step = pl.program_id(0)
    steps = pl.num_programs(0)
    rows_at = pl.multiple_of(step * MID, MID)
    here = pl.ds(rows_at, MID)
    chunk = 768
    weights = ((wout_all, wout_ref), (wup_all, wup_ref), (wdown_all, wdown_ref))
    loads = [pltpu.make_async_copy(a, b, load.at[i]) for i, (a, b) in enumerate(weights)]

    @pl.when(step == 0)
    def _():
        for copy in loads:
            copy.start()
        small24_ref[...] = jnp.zeros_like(small24_ref)
        small96_ref[...] = jnp.zeros_like(small96_ref)
        loads[0].wait()

    attended = o_ref[...]
    y1 = x_ref[...].astype(F32) + nn(attended, wout_ref[...]) + vec24_ref[2:3, :]
    normed, inverse = norm_parts(y1)
    h2 = (normed * vec24_ref[3:4, :] + vec24_ref[4:5, :]).astype(BF16)
    rows = lax.broadcasted_iota(jnp.int32, (MID, D), 0) + rows_at
    upstream = jnp.where(rows < len_ref[0], cot_ref[...].astype(F32), 0.0)
    upstream16 = upstream.astype(BF16)
    h2_t[:, here] = h2.T
    o_t[:, here] = attended.T
    dy[here, :] = upstream16
    small24_ref[5:6, :] += jnp.sum(upstream, axis=0, keepdims=True)

    @pl.when(step == 0)
    def _():
        loads[1].wait()
        loads[2].wait()

    y = y1 + vec24_ref[5:6, :]
    dh2 = None
    for c in range(FF // CHUNK):
        cols = slice(c * CHUNK, (c + 1) * CHUNK)
        u = nn(h2, wup_ref[:, cols]) + vec96_ref[7:8, cols]
        square = u * u
        t = jnp.tanh(u * (0.7978845608028654 + 0.035677408136300125 * square))
        half = 0.5 * (1.0 + t)
        f = (u * half).astype(BF16)
        slope = half + (0.5 * u) * (1.0 - t * t) * (
            0.7978845608028654 + 0.10703222440890037 * square
        )
        y = y + nn(f, wdown_ref[cols, :])
        df = nt(upstream16, wdown_ref[cols, :])
        d16 = (df * slope).astype(BF16)
        du[here, cols] = d16
        f_t[cols, here] = f.T
        small96_ref[7:8, cols] += jnp.sum(d16.astype(F32), axis=0, keepdims=True)
        part = nt(d16, wup_ref[:, cols])
        dh2 = part if c == 0 else dh2 + part
    mixed_ref[...] = y.astype(BF16)
    e = dh2 * vec24_ref[3:4, :]
    dy1 = dy[here, :].astype(F32) + norm_back(e, normed, inverse)
    dz16 = dy1.astype(BF16)
    dy1_ref[...] = dy1
    do_ref[...] = nt(dz16, wout_ref[...]).astype(BF16)
    small24_ref[2:3, :] += jnp.sum(dz16.astype(F32), axis=0, keepdims=True)
    small24_ref[3:4, :] += jnp.sum(dh2 * normed, axis=0, keepdims=True)
    small24_ref[4:5, :] += jnp.sum(dh2, axis=0, keepdims=True)
    dz[here, :] = dz16

    @pl.when(step == steps - 1)
    def _():
        shards = gout_ref.shape[0]

        def pipeline(count, stage, compute, target):
            def one(k, carry):
                slot = lax.rem(k, 2)
                copy = pltpu.make_async_copy(stage.at[slot], target(k), store.at[slot])

                @pl.when(k >= 2)
                def _():
                    copy.wait()

                stage[slot] = compute(k)
                copy.start()
                return carry

            lax.fori_loop(0, count, one, 0)
            for k in (count - 2, count - 1):
                pltpu.make_async_copy(stage.at[k % 2], target(k), store.at[k % 2]).wait()

        def blocks(value, depth):
            return value.reshape(value.shape[0] // depth, depth, value.shape[1]).astype(BF16)

        def block(k):
            return pl.ds(pl.multiple_of(k * chunk, chunk), chunk)

        pipeline(
            4,
            flat,
            lambda k: blocks(nn(f_t[block(k), :], dy[...]), D // shards),
            lambda k: gdown_ref.at[pl.ds(k * shards, shards)],
        )
        pipeline(
            4,
            flat,
            lambda k: blocks(nn(h2_t[...], du[:, block(k)]), D // shards),
            lambda k: gup_ref.at[:, :, block(k)],
        )
        flat[0] = blocks(nn(o_t[...], dz[...]), D // shards)
        last = pltpu.make_async_copy(flat.at[0], gout_ref, store.at[0])
        last.start()
        last.wait()


def middle_call(lengths, x, attended, cotangent, vec24, vec96, wout, wup, wdown, shards):
    length = x.shape[0]

    def rows(width):
        return pl.BlockSpec((MID, width), lambda i: (i, 0))

    def whole(shape):
        return pl.BlockSpec(shape, lambda i: (0,) * len(shape), pipeline_mode=pl.Buffered(1))

    anywhere = pl.BlockSpec(memory_space=pl.ANY)
    outs = (
        ((length, D), BF16, rows(D)),
        ((length, D), BF16, rows(D)),
        ((length, D), F32, rows(D)),
        ((shards, D // shards, D), BF16, anywhere),
        ((shards, D // shards, FF), BF16, anywhere),
        ((FF // D * shards, D // shards, D), BF16, anywhere),
        ((16, D), F32, whole((16, D))),
        ((16, FF), F32, whole((16, FF))),
    )
    return pl.pallas_call(
        middle_kernel,
        grid=(length // MID,),
        out_shape=tuple(jax.ShapeDtypeStruct(s, t) for s, t, _ in outs),
        in_specs=[
            pl.BlockSpec(memory_space=pltpu.SMEM),
            rows(D), rows(D), rows(D),
            whole(vec24.shape), whole(vec96.shape),
            anywhere, anywhere, anywhere,
        ],
        out_specs=tuple(b for _, _, b in outs),
        scratch_shapes=[
            VMEM((FF, length), BF16),
            VMEM((length, FF), BF16),
            VMEM((D, length), BF16),
            VMEM((length, D), BF16),
            VMEM((length, D), BF16),
            VMEM((D, length), BF16),
            VMEM(wout.shape, BF16),
            VMEM(wup.shape, BF16),
            VMEM(wdown.shape, BF16),
            VMEM((2, shards, D // shards, D), BF16),
            pltpu.SemaphoreType.DMA((3,)),
            pltpu.SemaphoreType.DMA((2,)),
        ],
        compiler_params=pltpu.CompilerParams(
            dimension_semantics=("arbitrary",), vmem_limit_bytes=63 * 2**20
        ),
    )(lengths, x, attended, cotangent, vec24, vec96, wout, wup, wdown)


def tail_rows(block, x_ref, dy1_ref, vec24_ref, wqkv_ref, dqkv_ref, h1_t, gx_ref, s24_ref, s72_ref):
    here = pl.ds(pl.multiple_of(block * BLK, BLK), BLK)
    normed, inverse = norm_parts(x_ref[here, :].astype(F32))
    if h1_t is not None:
        h1_t[:, here] = (normed * vec24_ref[0:1, :] + vec24_ref[1:2, :]).astype(BF16).T
    grad = dqkv_ref[here, :]
    dh1 = nt(grad, wqkv_ref[...])
    e = dh1 * vec24_ref[0:1, :]
    gx_ref[here, :] = (dy1_ref[here, :] + norm_back(e, normed, inverse)).astype(BF16)
    s24_ref[0:1, :] += jnp.sum(dh1 * normed, axis=0, keepdims=True)
    s24_ref[1:2, :] += jnp.sum(dh1, axis=0, keepdims=True)
    s72_ref[6:7, :] += jnp.sum(grad.astype(F32), axis=0, keepdims=True)


def backward_kernel(
    x_ref, dy1_ref, vec24_ref, wqkv_ref, qkv_ref, o_ref, do_ref, lse_ref,
    gx_ref, gqkv_ref, s24_ref, s72_ref,
    dqkv, h1_t, kt, dk, dv,
):
    s24_ref[...] = jnp.zeros_like(s24_ref)
    s72_ref[...] = jnp.zeros_like(s72_ref)
    lax.fori_loop(
        0,
        HEADS // 2,
        lambda p, c: (
            attention_back_pair(p, qkv_ref, o_ref, do_ref, lse_ref, dqkv, kt, dk, dv),
            c,
        )[1],
        0,
    )
    lax.fori_loop(
        0,
        x_ref.shape[0] // BLK,
        lambda b, c: (
            tail_rows(
                b, x_ref, dy1_ref, vec24_ref, wqkv_ref, dqkv, h1_t, gx_ref, s24_ref, s72_ref
            ),
            c,
        )[1],
        0,
    )
    shards = gqkv_ref.shape[0]
    many = shards // 4

    def one(i, carry):
        left = pl.ds(pl.multiple_of(i * (D // 4), D // 4), D // 4)
        for part in range(3):
            cols = slice(part * D, (part + 1) * D)
            value = nn(h1_t[left, :], dqkv[:, cols]).reshape(many, D // shards, D)
            gqkv_ref[pl.ds(i * many, many), :, cols] = value.astype(BF16)
        return carry

    lax.fori_loop(0, 4, one, 0)


def backward_call(x, dy1, vec24, wqkv, qkv, attended, grad_attended, lse, shards):
    length = x.shape[0]
    return pl.pallas_call(
        backward_kernel,
        out_shape=(
            jax.ShapeDtypeStruct((length, D), BF16),
            jax.ShapeDtypeStruct((shards, D // shards, 3 * D), BF16),
            jax.ShapeDtypeStruct((16, D), F32),
            jax.ShapeDtypeStruct((16, 3 * D), F32),
        ),
        in_specs=[pl.BlockSpec(memory_space=VMEM)] * 8,
        out_specs=(pl.BlockSpec(memory_space=VMEM),) * 4,
        scratch_shapes=[
            VMEM((length, 3 * D), BF16),
            VMEM((D, length), BF16),
            VMEM((128, length), BF16),
            VMEM((length, 128), F32),
            VMEM((length, 128), F32),
        ],
        compiler_params=pltpu.CompilerParams(vmem_limit_bytes=60 * 2**20),
    )(x, dy1, vec24, wqkv, qkv, attended, grad_attended, lse)


def place():
    wide = lax.axis_index("wide")
    return wide // 4, (wide // 2) % 2, wide % 2, lax.axis_index("narrow")


def device(z, x, c, y):
    return ((z * 2 + x) * 2 + c, y)


def greet():
    z, x, c, y = place()
    barrier = pltpu.get_barrier_semaphore()
    peers = [device(lax.rem(z + d, 4), x, c, y) for d in (1, 2, 3)]
    peers += [device(z, 1 - x, c, y), device(z, x, c, 1 - y), device(z, x, 1 - c, y)]
    for peer in peers:
        pl.semaphore_signal(barrier, inc=1, device_id=peer, device_id_type=MESH)
    pl.semaphore_wait(barrier, len(peers))


def remote(src, dst, sems, slot, peer):
    return pltpu.make_async_remote_copy(
        src_ref=src, dst_ref=dst, send_sem=sems[0].at[slot], recv_sem=sems[1].at[slot],
        device_id=peer, device_id_type=MESH,
    )


FIRST_Z = (("z", "x", "y"), ("z", "y", "x"))
LATER_Z = (("x", "z", "y"), ("y", "z", "x"))
UP_ORDERS = FIRST_Z
DOWN_ORDERS = LATER_Z


def peers_of(z, x, c, y):
    return {
        "z": [device(lax.rem(z + d, 4), x, c, y) for d in (1, 2, 3)],
        "x": [device(z, 1 - x, c, y)],
        "y": [device(z, x, c, 1 - y)],
        "c": [device(z, x, 1 - c, y)],
    }


def halves(low, high):
    cut = (high - low) // 256 * 128
    return [(low, low + cut), (low + cut, high)] if cut else [(low, high)]


def window(span):
    return pl.ds(span[0], span[1] - span[0])


class Gather:
    slots = 16

    def __init__(self, own, full, sems, local, rows=None, cols=None, orders=FIRST_Z):
        height, width = full.shape[-2:]
        span = cols or (0, width)
        rows = slice(None) if rows is None else window(rows)
        z, x, c, y = place()
        here = {"z": z, "x": x, "y": y}
        peers = peers_of(z, x, c, y)
        lanes = list(zip(halves(*span), orders))
        self.groups = [[], [], []]
        self.core = [[], [], [], []]
        slot = 0

        def at(state, cols):
            return full.at[state["z"], state["x"], c, state["y"], rows, window(cols)]

        for k in range(3):
            items = lanes
            if k == 0 and all(order[0] == orders[0][0] for _, order in lanes):
                items = [(span, orders[0])]
            for cols, order in items:
                now = {d: slice(None) if d in order[:k] else here[d] for d in "zxy"}
                source = own.at[rows, window(cols)] if k == 0 else at(now, cols)
                for peer in peers[order[k]]:
                    self.groups[k].append(remote(source, at(now, cols), sems, slot, peer))
                    slot += 1
                if "z" in order[: k + 1]:
                    later = dict(now)
                    later[order[k]] = slice(None) if order[k] == "z" else 1 - here[order[k]]
                    view = at(later, cols)
                    self.core[k + 1].append(remote(view, view, sems, slot, peers["c"][0]))
                    slot += 1
        self.kept = pltpu.make_async_copy(own.at[rows, window(span)], at(here, span), local)

    def run(self, stage):
        if stage == 0:
            self.kept.start()
        elif stage == 1:
            self.kept.wait()
        if 1 <= stage <= 3:
            for copy in self.groups[stage - 1]:
                copy.wait_recv()
        if stage <= 2:
            for copy in self.groups[stage]:
                copy.start()
        if stage <= 3:
            for copy in self.core[stage]:
                copy.start()
        every_core = [copy for copies in self.core for copy in copies]
        if stage == 4:
            for copy in every_core:
                copy.wait_recv()
        if stage == 5:
            for copy in every_core + [copy for copies in self.groups for copy in copies]:
                copy.wait_send()


def spread(blocks, each):
    width = 32 * each
    lane = lax.broadcasted_iota(jnp.int32, (128, width), 0)
    col = lax.broadcasted_iota(jnp.int32, (128, width), 1)
    value = nn(blocks, (lax.rem(col, each) == lane).astype(BF16)).reshape(32, 16, width)
    shard = lax.broadcasted_iota(jnp.int32, (32, 16, width), 0)
    col = lax.broadcasted_iota(jnp.int32, (32, 16, width), 2)
    inside = (col >= shard * each) & (col < shard * each + each)
    return jnp.sum(jnp.where(inside, value, 0.0), axis=0)


FORWARD = {
    "n": ("X0", "S0", "Y0",),
    "h": ("Z0", "X1", "S1", "O0", "X2", "U0", "S2", "Y1", "D0", "X3", "S3", "S4", "Y2",),
    0: ("X4", "Z1", "V0", "O1", "E0",),
    1: ("Y3", "Z2",),
    3: ("O2",),
    5: ("Z3", "U1", "D1",),
    8: ("O3",),
    9: ("V1",),
    10: ("Y4", "U2",),
    14: ("V2", "E1",),
    15: ("U3",),
    20: ("Z4", "D2",),
    21: ("V3",),
    24: ("E2",),
    25: ("D3",),
    "last": ("E3", "O4", "U4", "D4", "V4", "E4",),
}


def runner(parts, table):
    def run(at):
        for word in table.get(at, ()):
            parts[word[0]].run(int(word[1]))

    return run


def when_run(run, table, value, positions):
    for number, at in positions:
        if at in table:

            @pl.when(value == number)
            def _():
                run(at)


def gather_forward_kernel(
    x_ref, small_ref, wqkv_own, wout_own, wup_own, wdown_own,
    wqkv_out, wout_full, wup_full, wdown_full, vec24_ref, vec96_ref, qkv_out, o_out, lse_ref,
    small_full, wqkv_full, vec72, own_groups, hidden, vt, wqkv_ref, qkv_ref, o_ref,
    send, recv, local, store,
):
    greet()
    results = ((wqkv_ref, wqkv_out), (qkv_ref, qkv_out), (o_ref, o_out))
    stores = [pltpu.make_async_copy(a, b, store.at[i]) for i, (a, b) in enumerate(results)]
    length = x_ref.shape[0]
    steps = length // BLK
    half = wdown_full.shape[-2] // 2
    parts = {}

    def add_part(name, own, full, **view):
        i = len(parts)
        parts[name] = Gather(own, full, (send.at[i], recv.at[i]), local.at[i], **view)

    add_part("S", small_ref, small_full)
    for group, name in enumerate("XYZ"):
        add_part(name, own_groups, wqkv_full, cols=(group * D, (group + 1) * D))
        for part in range(3):
            own_groups[:, (3 * group + part) * 256 : (3 * group + part + 1) * 256] = wqkv_own[
                :, part * D + group * 256 : part * D + (group + 1) * 256
            ]
    add_part("O", wout_own, wout_full)
    add_part("U", wup_own, wup_full, cols=(0, FF // 2), orders=UP_ORDERS)
    add_part("V", wup_own, wup_full, cols=(FF // 2, FF), orders=UP_ORDERS)
    add_part("D", wdown_own, wdown_full, rows=(0, half), orders=DOWN_ORDERS)
    add_part("E", wdown_own, wdown_full, rows=(half, 2 * half), orders=DOWN_ORDERS)
    run = runner(parts, FORWARD)
    run("n")

    def normalize(block, carry):
        here = pl.ds(pl.multiple_of(block * BLK, BLK), BLK)
        normed, _ = norm_parts(x_ref[here, :].astype(F32))
        hidden[here, :] = (normed * vec24_ref[0:1, :] + vec24_ref[1:2, :]).astype(BF16)
        return carry

    run("h")
    blocks = small_full[...].reshape(32 * 16, 128)
    for ref, each in zip((vec24_ref, vec72, vec96_ref), (24, 72, 96)):
        ref[...] = spread(blocks, each)
    lax.fori_loop(0, steps, normalize, 0)

    def group_qkv(group):
        wide = pl.ds(pl.multiple_of(group * D, D), D)

        def spot(part):
            return pl.ds(pl.multiple_of(part * D + group * 256, 256), 256)

        def flatten(i, carry):
            two = wqkv_full[i // 4, (i // 2) % 2, i % 2, :, :, wide].astype(F32)
            two = two.reshape(D // 16, D).astype(BF16)
            rows = pl.ds(pl.multiple_of(i * (D // 16), D // 16), D // 16)
            for part in range(3):
                wqkv_ref[rows, spot(part)] = two[:, part * 256 : (part + 1) * 256]
            return carry

        lax.fori_loop(0, 16, flatten, 0)

        def rows_qkv(block, carry):
            here = pl.ds(pl.multiple_of(block * BLK, BLK), BLK)
            for part in range(3):
                value = nn(hidden[here, :], wqkv_ref[:, spot(part)]) + vec72[6:7, spot(part)]
                qkv_ref[here, spot(part)] = value.astype(BF16)
            return carry

        lax.fori_loop(0, steps, rows_qkv, 0)

    def one(pair, carry):
        def event(j):
            spots = [(p, p * (steps + 1) + 1 + j) for p in range(HEADS // 2)]
            when_run(run, FORWARD, pair, spots)

        event(-1)

        @pl.when(pair % 2 == 0)
        def _():
            group_qkv(pair // 2)

        attention_pair(pair, qkv_ref, o_ref, lse_ref, vt, event)
        return carry

    lax.fori_loop(0, HEADS // 2, one, 0)
    for copy in stores:
        copy.start()
    run("last")
    for part in parts.values():
        part.run(5)
    for copy in stores:
        copy.wait()


def gather_forward_call(x, small, wqkv, wout, wup, wdown):
    length = x.shape[0]
    anywhere = pl.BlockSpec(memory_space=pl.ANY)
    inside = pl.BlockSpec(memory_space=VMEM)

    def full(own):
        return jax.ShapeDtypeStruct((4, 2, 2, 2, *own.shape), BF16)

    return pl.pallas_call(
        gather_forward_kernel,
        out_shape=(
            jax.ShapeDtypeStruct((D, 3 * D), BF16),
            full(wout), full(wup), full(wdown),
            jax.ShapeDtypeStruct((16, D), F32),
            jax.ShapeDtypeStruct((16, FF), F32),
            jax.ShapeDtypeStruct((length, 3 * D), BF16),
            jax.ShapeDtypeStruct((length, D), BF16),
            jax.ShapeDtypeStruct((HEADS // 2, 8, length), F32),
        ),
        in_specs=[inside] * 3 + [anywhere] * 3,
        out_specs=(*[anywhere] * 4, inside, inside, anywhere, anywhere, inside),
        scratch_shapes=[
            VMEM((4, 2, 2, 2, 16, 128), BF16),
            VMEM((4, 2, 2, 2, *wqkv.shape), BF16),
            VMEM((16, 3 * D), F32),
            VMEM(wqkv.shape, BF16),
            VMEM((length, D), BF16),
            VMEM((128, length), BF16),
            VMEM((D, 3 * D), BF16),
            VMEM((length, 3 * D), BF16),
            VMEM((length, D), BF16),
            pltpu.SemaphoreType.DMA((9, Gather.slots)),
            pltpu.SemaphoreType.DMA((9, Gather.slots)),
            pltpu.SemaphoreType.DMA((9,)),
            pltpu.SemaphoreType.DMA((3,)),
        ],
        compiler_params=pltpu.CompilerParams(
            collective_id=1, has_side_effects=True, vmem_limit_bytes=60 * 2**20
        ),
    )(x, small, wqkv, wout, wup, wdown)


SIZES = {"z": 4, "x": 2, "y": 2}


def held_after(order, k):
    return [d for d in "zxy" if d not in order[:k]]


class Scatter:
    slots = 12

    def __init__(self, grads, buffers, sems, local, put, rows=None, cols=None, orders=FIRST_Z):
        height, width = grads.shape[-2:]
        low, high = cols or (0, width)
        rows = slice(None) if rows is None else window(rows)
        cols = slice(None) if cols is None else window(cols)
        z, x, c, y = place()
        self.here = {"z": z, "x": x, "y": y}
        self.core_at = c
        peers = peers_of(z, x, c, y)
        self.grads, self.put = grads, put
        self.mine, self.one, *rest = buffers
        if self.mine is not None:
            self.kept = pltpu.make_async_copy(grads.at[:, :, c, :, rows, cols], self.mine, local)
        self.groups = [[remote(grads.at[:, :, 1 - c, :, rows, cols], self.one, sems, 0, peers["c"][0])]]
        self.groups += [[], [], []]
        self.lanes = []
        slot = 1
        for span, order in zip(halves(0, high - low), orders):
            order = order[::-1]
            got = [rest.pop(0) for _ in range(3)]
            self.lanes.append((window(span), order, got))
            for k in range(3):
                source = self.one if k == 0 else got[k - 1]
                cut = (slice(None), window(span)) if k == 0 else (slice(None), slice(None))
                if k > 0 and order[k - 1] == "z":
                    source = source.at[0]
                if order[k] == "z":
                    others = [lax.rem(z + d, 4) for d in (1, 2, 3)]
                else:
                    others = [1 - self.here[order[k]]]
                for i, (other, peer) in enumerate(zip(others, peers[order[k]])):
                    index = [other if d == order[k] else slice(None) for d in held_after(order, k)]
                    target = got[k].at[i] if order[k] == "z" else got[k]
                    self.groups[k + 1].append(
                        remote(source.at[(*index, *cut)], target, sems, slot, peer)
                    )
                    slot += 1

    @staticmethod
    def shapes(r, n, mine, orders=FIRST_Z):
        result = [VMEM((4, 2, 2, r, n), BF16)] * (2 if mine else 1)
        for (low, high), order in zip(halves(0, n), orders):
            order = order[::-1]
            for k in range(3):
                held = [SIZES[d] for d in held_after(order, k + 1)]
                lead = [3] if order[k] == "z" else []
                result.append(VMEM((*lead, *held, r, high - low), BF16))
        return result

    def add(self, lane, k):
        cols, order, got = lane
        before = held_after(order, k)
        after = held_after(order, k + 1)

        def total(index):
            at = dict(zip(after, index))
            at[order[k]] = self.here[order[k]]
            where = tuple(at[d] for d in before)
            if k == 0:
                value = self.one[(*where, slice(None), cols)]
            else:
                lead = (0,) if order[k - 1] == "z" else ()
                value = got[k - 1][(*lead, *where)]
            lead = [(i,) for i in range(3)] if order[k] == "z" else [()]
            if k == 2:
                value = value.astype(F32)
                for i in lead:
                    value = value + got[k][i + index].astype(F32)
                return value
            for i in lead:
                value = value + got[k][i + index]
            got[k][lead[0] + index] = value

        if not after:
            return total(())
        sizes = [SIZES[d] for d in after]

        def loop(i, carry):
            if len(sizes) == 1:
                total((i,))
            else:
                for j in range(sizes[1]):
                    total((i, j))
            return carry

        lax.fori_loop(0, sizes[0], loop, 0)

    def run(self, stage):
        if stage == 0 and self.mine is not None:
            self.kept.start()
        if stage == 1 and self.mine is not None:
            self.kept.wait()
        if 1 <= stage <= 4:
            for copy in self.groups[stage - 1]:
                copy.wait_recv()
        if stage == 1:

            def add(i, carry):
                a, b = i // 2, i % 2
                own = self.grads[a, b, self.core_at] if self.mine is None else self.mine[a, b]
                self.one[a, b] = self.one[a, b] + own
                return carry

            lax.fori_loop(0, 8, add, 0)
        if stage in (2, 3):
            for lane in self.lanes:
                self.add(lane, stage - 2)
        if stage == 4:
            values = [self.add(lane, 2) for lane in self.lanes]
            self.put(values[0] if len(values) == 1 else jnp.concatenate(values, axis=1))
        if stage <= 3:
            for copy in self.groups[stage]:
                copy.start()
        if stage == 5:
            for copies in self.groups:
                for copy in copies:
                    copy.wait_send()


def fold(values, each, row):
    width = 32 * each
    shard = lax.broadcasted_iota(jnp.int32, (32, 16, width), 0)
    col = lax.broadcasted_iota(jnp.int32, (32, 16, width), 2)
    inside = (col >= shard * each) & (col < shard * each + each)
    spreaded = jnp.where(inside, values[None], 0.0).reshape(32 * 16, width).astype(BF16)
    lane = lax.broadcasted_iota(jnp.int32, (128, width), 0)
    col = lax.broadcasted_iota(jnp.int32, (128, width), 1)
    return nt(spreaded, (lax.rem(col, each) == lane).astype(BF16))


BACKWARD = {
    "h": ("D0", "E0", "U0",),
    0: ("V0", "O0",),
    1: ("D1",),
    5: ("E1",),
    6: ("D2",),
    "g0": ("X0", "U1",),
    10: ("V1",),
    12: ("E2",),
    14: ("D3", "U2",),
    "g1": ("V2", "Y0",),
    17: ("O1", "U3",),
    18: ("X1",),
    20: ("E3",),
    21: ("V3", "O2", "X2",),
    22: ("Y1",),
    23: ("O3",),
    "t0": ("Z0",),
    "t1": ("X3", "Y2", "Z1",),
    "t3": ("Y3",),
    "f": ("Z2",),
    "e": ("S0",),
    "last": ("S1", "Z3", "S2", "S3", "D4", "E4", "U4", "V4", "O4", "X4", "Y4", "Z4", "S4",),
}
GROUPS = 3


def scatter_backward_kernel(
    x_all, dy1_all, vec24_ref, wqkv_all, qkv_all, o_all, do_all, lse_ref, s24_mid, s96_mid,
    gout_all, gup_all, gdown_all,
    gx_ref, gqkv_ref, gout_ref, gup_ref, gdown_ref, small_ref,
    dqkv, h1_t, kt, dk, dv, s24_ref, s72_ref, small_all,
    x_ref, qkv_ref, do_ref, o_ref, dy1_ref, wqkv_ref, *buffers,
):
    send, recv, local, load = buffers[-4:]
    buffers = list(buffers[:-4])
    greet()
    inputs = (
        (x_all, x_ref), (qkv_all, qkv_ref), (do_all, do_ref), (o_all, o_ref), (dy1_all, dy1_ref),
        (wqkv_all, wqkv_ref),
    )
    loads = [pltpu.make_async_copy(a, b, load.at[i]) for i, (a, b) in enumerate(inputs)]
    half = gdown_all.shape[-2] // 2
    parts = {}

    def add_part(name, grads, mine, put, **view):
        i = len(parts)
        held = [buffers.pop(0)] if mine else [None]
        count = 4 if len(halves(0, grads.shape[-1])) == 1 else 7
        held += [buffers.pop(0) for _ in range(count)]
        parts[name] = Scatter(grads, held, (send.at[i], recv.at[i]), local.at[i], put, **view)

    def put_at(ref, rows, cols):
        def put(value):
            ref[rows, cols] = value

        return put

    every = slice(None)
    for name, k in (("U", 0), ("V", 1)):
        cols = (k * FF // 2, (k + 1) * FF // 2)
        add_part(name, gup_all, True, put_at(gup_ref, every, slice(*cols)), cols=cols, orders=UP_ORDERS)
    for name, k in (("D", 0), ("E", 1)):
        rows = (k * half, (k + 1) * half)
        add_part(name, gdown_all, True, put_at(gdown_ref, slice(*rows), every), rows=rows, orders=DOWN_ORDERS)
    add_part("O", gout_all, True, put_at(gout_ref, every, every))
    groups = [buffers.pop(0) for _ in range(GROUPS)]

    def put_group(group):
        def put(value):
            for part in range(3):
                low = part * D + group * 256
                gqkv_ref[:, low : low + 256] = value[:, part * 256 : (part + 1) * 256]

        return put

    for group, name in enumerate("XYZ"):
        add_part(name, groups[group], False, put_group(group))
    add_part("S", small_all, False, put_at(small_ref, every, every))

    run = runner(parts, BACKWARD)
    run("h")
    for copy in loads:
        copy.start()
    s24_ref[...] = jnp.zeros_like(s24_ref)
    s72_ref[...] = jnp.zeros_like(s72_ref)
    length = x_ref.shape[0]
    steps = length // BLK

    def hidden_rows(block, carry):
        here = pl.ds(pl.multiple_of(block * BLK, BLK), BLK)
        normed, _ = norm_parts(x_ref[here, :].astype(F32))
        hidden = (normed * vec24_ref[0:1, :] + vec24_ref[1:2, :]).astype(BF16)
        h1_t[:, here] = hidden.T
        return carry

    loads[0].wait()
    lax.fori_loop(0, steps, hidden_rows, 0)
    for copy in loads[1:4]:
        copy.wait()

    def group_grads(group):
        def one(i, carry):
            left = pl.ds(pl.multiple_of(i * (D // 4), D // 4), D // 4)
            for part in range(3):
                low = part * D + group * 256
                value = nn(h1_t[left, :], dqkv[:, low : low + 256])
                value = value.reshape(2, 2, 2, D // 32, 256).astype(BF16)
                groups[group][i, :, :, :, :, part * 256 : (part + 1) * 256] = value
            return carry

        lax.fori_loop(0, 4, one, 0)

    def one(pair, carry):
        def event(j):
            at_step = steps - 1 - j
            if at_step == 0:
                for group in range(GROUPS - 1):

                    @pl.when(pair == 2 * group + 2)
                    def _():
                        group_grads(group)
                        run(f"g{group}")

            spots = [(p, p * steps + at_step) for p in range(HEADS // 2)]
            when_run(run, BACKWARD, pair, spots)

        attention_back_pair(pair, qkv_ref, o_ref, do_ref, lse_ref, dqkv, kt, dk, dv, event)
        return carry

    lax.fori_loop(0, HEADS // 2, one, 0)
    run("g2")
    group_grads(GROUPS - 1)
    for copy in loads[4:]:
        copy.wait()

    def tail(block, carry):
        when_run(run, BACKWARD, block, [(b, f"t{b}") for b in range(steps)])
        tail_rows(block, x_ref, dy1_ref, vec24_ref, wqkv_ref, dqkv, None, gx_ref, s24_ref, s72_ref)
        return carry

    lax.fori_loop(0, steps, tail, 0)
    run("f")
    total = fold(s24_ref[...] + s24_mid[...], 24, 0)
    total = total + fold(s72_ref[...], 72, 6) + fold(s96_mid[...], 96, 7)
    small_all[...] = total.reshape(4, 2, 2, 2, 16, 128).astype(BF16)
    run("e")
    run("last")
    for part in parts.values():
        part.run(5)


def scatter_backward_call(
    x, dy1, vec24, wqkv, qkv, attended, grad_attended, lse, s24, s96, gout, gup, gdown
):
    length = x.shape[0]
    anywhere = pl.BlockSpec(memory_space=pl.ANY)
    inside = pl.BlockSpec(memory_space=VMEM)
    deep = gdown.shape[-2]
    scratch = [
        VMEM((length, 3 * D), BF16),
        VMEM((D, length), BF16),
        VMEM((128, length), BF16),
        VMEM((length, 128), F32),
        VMEM((length, 128), F32),
        VMEM((16, D), F32),
        VMEM((16, 3 * D), F32),
        VMEM((4, 2, 2, 2, 16, 128), BF16),
        VMEM((length, D), BF16),
        VMEM((length, 3 * D), BF16),
        VMEM((length, D), BF16),
        VMEM((length, D), BF16),
        VMEM((length, D), F32),
        VMEM((D, 3 * D), BF16),
    ]
    for _ in range(2):
        scratch += Scatter.shapes(D // 32, FF // 2, True, UP_ORDERS)
    for _ in range(2):
        scratch += Scatter.shapes(deep // 2, D, True, DOWN_ORDERS)
    scratch += Scatter.shapes(D // 32, D, True)
    scratch += [VMEM((4, 2, 2, 2, D // 32, D), BF16)] * GROUPS
    for _ in range(GROUPS):
        scratch += Scatter.shapes(D // 32, D, False)
    scratch += Scatter.shapes(16, 128, False)
    scratch += [pltpu.SemaphoreType.DMA((9, Scatter.slots))] * 2 + [pltpu.SemaphoreType.DMA((9,))]
    scratch += [pltpu.SemaphoreType.DMA((6,))]
    return pl.pallas_call(
        scatter_backward_kernel,
        out_shape=(
            jax.ShapeDtypeStruct((length, D), BF16),
            jax.ShapeDtypeStruct((D // 32, 3 * D), F32),
            jax.ShapeDtypeStruct((D // 32, D), F32),
            jax.ShapeDtypeStruct((D // 32, FF), F32),
            jax.ShapeDtypeStruct((deep, D), F32),
            jax.ShapeDtypeStruct((16, 128), F32),
        ),
        in_specs=[
            anywhere, anywhere, inside, *[anywhere] * 4, inside, inside, inside, *[anywhere] * 3
        ],
        out_specs=(inside,) * 6,
        scratch_shapes=scratch,
        compiler_params=pltpu.CompilerParams(
            collective_id=2, has_side_effects=True, vmem_limit_bytes=63 * 2**20
        ),
    )(x, dy1, vec24, wqkv, qkv, attended, grad_attended, lse, s24, s96, gout, gup, gdown)


def pack_kernel(*refs):
    *vectors, out, rows = refs
    rows[...] = jnp.zeros_like(rows)
    for row, vector in enumerate(vectors):
        rows[row, 0 : vector.shape[0]] = vector[...].astype(F32)
    out[...] = rows[...].astype(BF16)


def pack_call(vectors):
    inside = pl.BlockSpec(memory_space=VMEM)
    return pl.pallas_call(
        pack_kernel,
        out_shape=jax.ShapeDtypeStruct((16, 128), BF16),
        in_specs=[inside] * len(vectors),
        out_specs=inside,
        scratch_shapes=[VMEM((16, 128), F32)],
    )(*vectors)


def finish_kernel(
    gx, gqkv, gout, gup, gdown, small, gx_out, gqkv_out, gout_out, gup_out, gdown_out, *vectors
):
    gx_out[...] = gx[...]
    gqkv_out[...] = gqkv[...]
    gout_out[...] = gout[...]
    gup_out[...] = gup[...]
    gdown_out[...] = gdown[...]
    for row, out in enumerate(vectors):
        out[...] = small[row, 0 : out.shape[0]]


def finish_call(mixed, gx, gqkv, gout, gup, gdown, small, shapes):
    inside = pl.BlockSpec(memory_space=VMEM)
    whole = (gqkv, gout, gup, gdown)
    outs = [jax.ShapeDtypeStruct(gx.shape, gx.dtype)]
    outs += [jax.ShapeDtypeStruct(a.shape, F32) for a in whole]
    outs += [jax.ShapeDtypeStruct(shape, F32) for shape in shapes]
    gx, gqkv, gout, gup, gdown, *folded = pl.pallas_call(
        finish_kernel,
        out_shape=tuple(outs),
        in_specs=[inside] * 6,
        out_specs=(inside,) * len(outs),
        compiler_params=pltpu.CompilerParams(vmem_limit_bytes=60 * 2**20),
    )(gx, *whole, small)
    return (
        mixed, gx, folded[0], folded[1], gqkv, folded[6], gout, folded[2], folded[3], folded[4],
        gup, folded[7], gdown, folded[5],
    )


def shards(
    tokens, cotangent, lengths, ln1_gain, ln1_shift, qkv_weight, qkv_bias, out_weight, out_bias,
    ln2_gain, ln2_shift, up_weight, up_bias, down_weight, down_bias, *, special,
):
    vectors = (ln1_gain, ln1_shift, out_bias, ln2_gain, ln2_shift, down_bias, qkv_bias, up_bias)
    if special:
        small = pack_call(vectors)
        wqkv, wout, wup, wdown, vec24, vec96, qkv, attended, lse = gather_forward_call(
            tokens, small, qkv_weight, out_weight, up_weight, down_weight
        )
        wout, wup = (w.reshape(D, w.shape[-1]) for w in (wout, wup))
        wdown = wdown.reshape(FF, D)
    else:
        gather = functools.partial(lax.all_gather, axis_name=AXES, axis=0, tiled=True)
        wqkv, wout, wup, wdown = map(gather, (qkv_weight, out_weight, up_weight, down_weight))
        whole = [gather(v).astype(F32) for v in vectors]
        vec24 = jnp.pad(jnp.stack(whole[:6]), ((0, 10), (0, 0)))
        vec72 = jnp.pad(whole[6][None], ((6, 9), (0, 0)))
        vec96 = jnp.pad(whole[7][None], ((7, 8), (0, 0)))
        qkv, attended, lse = forward_call(tokens, vec24, vec72, wqkv)
    mixed, do, dy1, gout, gup, gdown, s24_mid, s96 = middle_call(
        lengths, tokens, attended, cotangent, vec24, vec96, wout, wup, wdown, 32
    )
    if special:
        gout, gup = (g.reshape(4, 2, 2, 2, *g.shape[1:]) for g in (gout, gup))
        gdown = gdown.reshape(4, 2, 2, 2, FF // 32, D)
        gx, gqkv, gout, gup, gdown, small = scatter_backward_call(
            tokens, dy1, vec24, wqkv, qkv, attended, do, lse, s24_mid, s96, gout, gup, gdown
        )
        return finish_call(mixed, gx, gqkv, gout, gup, gdown, small, [v.shape for v in vectors])
    else:
        gx, gqkv, s24, s72 = backward_call(tokens, dy1, vec24, wqkv, qkv, attended, do, lse, 32)
        scatter = functools.partial(
            lax.psum_scatter, axis_name=AXES, scatter_dimension=0, tiled=True
        )
        gqkv, gout, gup = (scatter(g.reshape(D, -1).astype(F32)) for g in (gqkv, gout, gup))
        gdown = scatter(gdown.reshape(FF, D).astype(F32))
        both = s24 + s24_mid
        folded = [scatter(both[i]) for i in range(6)] + [scatter(s72[6]), scatter(s96[7])]
    return (
        mixed, gx, folded[0], folded[1], gqkv, folded[6], gout, folded[2], folded[3], folded[4],
        gup, folded[7], gdown, folded[5],
    )


def solution(mesh):
    flat, rows = P(AXES), P(AXES, None)
    in_specs = (
        rows, rows, flat, flat, flat, rows, flat, rows, flat, flat, flat, rows, flat, rows, flat,
    )
    out_specs = (
        rows, rows, flat, flat, rows, flat, rows, flat, flat, flat, rows, flat, rows, flat,
    )
    special = dict(mesh.shape) == {"wide": 16, "narrow": 2}
    return jax.shard_map(
        functools.partial(shards, special=special),
        mesh=mesh, in_specs=in_specs, out_specs=out_specs, check_vma=False,
    )
```
